32 devices in a mesh: segment: 4 (over y, core), frame: 8 (over z, x).
Axes of the slice: x: 2, y: 2, z: 4, core: 2. Of those that a mesh axis runs over, the one named last changes fastest.
Arguments:
- clips: bfloat16 [4, 8, 320, 1024], P('segment', 'frame'), may hold values from -6 to 6
- timesteps: int32 [4], replicated, may hold values from 0 to 999
- gain: float32 [4, 320], replicated, may hold values from 0.25 to 1.75
- temporal_weight: bfloat16 [4, 3, 320, 320], P('segment'), may hold values from -0.1875 to 0.1875
- film_weight: bfloat16 [4, 320, 320], P('segment'), may hold values from -0.3125 to 0.3125
- out_weight: bfloat16 [4, 320, 320], P('segment'), may hold values from -0.3125 to 0.3125
- skip_weight: bfloat16 [2, 320, 320], replicated, may hold values from -0.3125 to 0.3125
Outputs:
- video_out: bfloat16 [4, 8, 320, 1024], P('segment', 'frame')
The draws below stay inside these ranges and needn't reach their ends.
All inputs are finite; a program needn't handle non-finite values.
Results may differ from the reference program's by a relative error of at most 0.012.
Values may be sent and summed in bfloat16 or wider, within the bound.
No kernel may reach another device: no remote copies, remote signals or barrier semaphores. Data moves between devices by JAX's collectives and lax.ppermute only.
A program may use at most 64 MiB of HBM per device.

```python
import math
import jax
import jax.numpy as jnp
from jax import lax

C = 320
PIX = 1024
MB = 4
FRAMES = 8


def with_ends(drawn, key, low, high):
    extent = drawn.shape
    place = [jax.random.randint(jax.random.fold_in(key, axis), (), 0, extent[axis]) for axis in range(len(extent))]
    drawn = drawn.at[tuple(place)].set(low)
    longest = extent.index(max(extent))
    place[longest] = (place[longest] + 1) % extent[longest]
    return drawn.at[tuple(place)].set(high)


def shard_levels(own_key, shape, cuts, low, high):
    loudness = 1.0
    for dim, shards_of in cuts:
        steps = jax.random.uniform(jax.random.fold_in(jax.random.fold_in(own_key, 6), dim), (shards_of,), jnp.float32, low / len(cuts), high / len(cuts))
        loudness = loudness * jnp.repeat(jnp.exp(steps), shape[dim] // shards_of).reshape((-1,) + (1,) * (len(shape) - 1 - dim))
    return loudness


def centred(stream_key, shape, deviation, bound, cuts=(), held_as=jnp.bfloat16):
    result = jax.random.normal(stream_key, shape, jnp.float32) * deviation
    if len(cuts) > 0:
        result = shard_levels(stream_key, shape, cuts, -0.22, 0.18) * result
    return jnp.clip(result, min=-bound, max=bound).astype(held_as)


def setup_inputs(seed: int = 0) -> dict:
    arg_keys = jax.random.split(jax.random.key(seed), 8)
    clips = centred(arg_keys[0], (MB, FRAMES, C, PIX), 1.0, 6.0, ((0, 4), (1, 8)))
    timesteps = with_ends(jax.random.randint(arg_keys[1], (MB,), 0, 1000), jax.random.fold_in(arg_keys[1], 1), 0, 999).astype(jnp.int32)
    gain = jnp.clip(1.0 + 0.15 * jax.random.normal(arg_keys[2], (MB, C), jnp.float32), 0.25, 1.75)
    temporal_weight = centred(arg_keys[3], (MB, 3, C, C), (3 * C) ** -0.5, 0.1875, ((0, 4),))
    film_weight = centred(arg_keys[4], (MB, C, C), C ** -0.5, 0.3125, ((0, 4),))
    out_weight = centred(arg_keys[5], (MB, C, C), C ** -0.5, 0.3125, ((0, 4),))
    skip_weight = centred(arg_keys[6], (2, C, C), C ** -0.5, 0.3125)
    return {"clips": clips, "timesteps": timesteps, "gain": gain, "temporal_weight": temporal_weight, "film_weight": film_weight, "out_weight": out_weight, "skip_weight": skip_weight}


def embed(timesteps, width):
    half = width // 2
    freq = jnp.exp(-math.log(10000.0) * jnp.arange(half, dtype=jnp.float32) / half)
    angle = timesteps.astype(jnp.float32)[:, None] * freq[None, :]
    return jnp.concatenate([jnp.sin(angle), jnp.cos(angle)], axis=-1).astype(jnp.bfloat16)

def reference(clips, timesteps, gain, temporal_weight, film_weight, out_weight, skip_weight):
    emb = embed(timesteps, C)
    frames = clips.shape[1]
    outputs = []
    state = clips
    for section in range(4):
        film = jnp.dot(emb, film_weight[section], preferred_element_type=jnp.float32)
        values = state.astype(jnp.float32)
        meansq = lax.optimization_barrier(jnp.mean(values * values, axis=2, keepdims=True))
        normed = (values * jax.lax.rsqrt(meansq + 1e-05) * gain[section][None, None, :, None]).astype(jnp.bfloat16)
        padded = jnp.pad(normed, ((0, 0), (1, 1), (0, 0), (0, 0))).astype(jnp.float32)
        mixed = jnp.zeros(values.shape, jnp.float32)
        for tap in range(3):
            mixed = mixed + jnp.einsum('io,mfip->mfop', temporal_weight[section, tap].astype(jnp.float32), padded[:, tap:tap + frames])
        hidden = jax.nn.silu(mixed * (1.0 + film[:, None, :, None])).astype(jnp.bfloat16)
        total = values + jnp.einsum('io,mfip->mfop', out_weight[section].astype(jnp.float32), hidden.astype(jnp.float32))
        if section == 2:
            total = total + jnp.einsum('io,mfip->mfop', skip_weight[0].astype(jnp.float32), outputs[0].astype(jnp.float32))
        if section == 3:
            total = total + jnp.einsum('io,mfip->mfop', skip_weight[1].astype(jnp.float32), clips.astype(jnp.float32))
        state = total.astype(jnp.bfloat16)
        outputs.append(state)
    return state
```

```python
import functools
import math

import jax
import jax.numpy as jnp
from jax import lax
from jax.experimental import pallas as pl
from jax.experimental.pallas import tpu as pltpu
from jax.sharding import PartitionSpec as P

BF = jnp.bfloat16
F32 = jnp.float32
LANES = 128
EPS = 1e-05


def embed(timesteps, width):
    half = width // 2
    freq = jnp.exp(-math.log(10000.0) * jnp.arange(half, dtype=jnp.float32) / half)
    angle = timesteps.astype(jnp.float32)[:, None] * freq[None, :]
    return jnp.concatenate([jnp.sin(angle), jnp.cos(angle)], axis=-1).astype(jnp.bfloat16)


def exchange(array, axis, by):
    return lax.ppermute(array, axis, [(i, i ^ by) for i in range(lax.axis_size(axis))])


def plain_section(state, gain, taps, film, projection, extra):
    values = state.astype(F32)
    meansq = jnp.mean(values * values, axis=1, keepdims=True)
    normed = (values * lax.rsqrt(meansq + EPS) * gain[None, :, None]).astype(BF)
    padded = jnp.pad(normed, ((1, 1), (0, 0), (0, 0)))
    count = state.shape[0]
    mixed = sum(
        jnp.einsum("io,fip->fop", taps[tau], padded[tau : tau + count], preferred_element_type=F32)
        for tau in range(3)
    )
    hidden = jax.nn.silu(mixed * (1.0 + film[None, :, None])).astype(BF)
    total = values + jnp.einsum("io,fip->fop", projection, hidden, preferred_element_type=F32)
    if extra is not None:
        total = total + jnp.einsum("io,fip->fop", extra[0], extra[1], preferred_element_type=F32)
    return total.astype(BF)


def plain_shards(clips, timesteps, gain, temporal_weight, film_weight, out_weight, skip_weight):
    own = clips[0]
    pixels = own.shape[2]
    split = lax.axis_size("frame")
    pad = -pixels % split
    if pad:
        own = jnp.pad(own, ((0, 0), (0, 0), (0, pad)))
    state = lax.all_to_all(own, "frame", 2, 0, tiled=True)
    emb = embed(timesteps, clips.shape[2])
    film = jnp.dot(emb, film_weight[0], preferred_element_type=F32)
    taps = lax.all_gather(temporal_weight[0], "segment")
    projection = lax.all_gather(out_weight[0], "segment")
    films = lax.all_gather(film, "segment")
    micro = lax.axis_index("segment")
    first = state
    skips = {}
    for section in range(gain.shape[0]):
        extra = None
        if section == 2:
            extra = (skip_weight[0], skips[0])
        if section == 3:
            extra = (skip_weight[1], first)
        film_vec = lax.dynamic_index_in_dim(films[section], micro, 0, keepdims=False)
        state = plain_section(
            state, gain[section], taps[section], film_vec, projection[section], extra
        )
        skips[section] = state
    result = lax.all_to_all(state, "frame", 0, 2, tiled=True)
    return result[None, :, :, :pixels]


def transposed_dot(weight, field):
    return lax.dot_general(weight, field, (((0,), (0,)), ((), ())), preferred_element_type=F32)


def sections_kernel(frames, width, *refs):
    blocks = refs[0:frames]
    taps_in = refs[frames : frames + 4]
    rest_in = refs[frames + 4 : frames + 8]
    skip_in, gain_ref = refs[frames + 8 : frames + 10]
    outs = refs[frames + 10 : 2 * frames + 10]
    first, taps, rest, skip, unfolded, one, work, last, sem_x, sem_w, sem_s, sem_o = refs[
        2 * frames + 10 :
    ]
    me = lax.axis_index("frame")
    segment = lax.axis_index("segment")
    columns = frames * LANES

    loads = [
        pltpu.make_async_copy(blocks[d], first.at[me ^ d], sem_x.at[d]) for d in range(frames)
    ]
    for load in loads:
        load.start()
    for b in range(4):
        to = segment ^ b
        pltpu.make_async_copy(taps_in[b], taps.at[to], sem_w.at[to, 0]).start()
        pltpu.make_async_copy(rest_in[b], rest.at[to], sem_w.at[to, 1]).start()
    skip_load = pltpu.make_async_copy(skip_in, skip, sem_s)
    skip_load.start()

    zeros = jnp.zeros((width, LANES), BF)
    for half in range(2):
        unfolded[half, 0:width, 0:LANES] = zeros
        unfolded[half, 2 * width :, columns - LANES :] = zeros
    chosen = lax.broadcasted_iota(jnp.int32, (16, LANES), 0)
    chosen = jnp.where((chosen == segment) | (chosen == segment + 4), 1.0, 0.0).astype(BF)
    for load in loads:
        load.wait()

    def at(ref, f):
        return ref[f] if ref is first else ref[:, f * LANES : (f + 1) * LANES]

    def pair(ref, j):
        return jnp.concatenate([at(ref, 2 * j), at(ref, 2 * j + 1)], axis=1)

    for s in range(4):
        source = (first, one, work, work)[s]
        target = (one, work, work, last)[s]
        half = s % 2
        for f in range(frames):
            values = at(source, f).astype(F32)
            scale = lax.rsqrt(jnp.mean(values * values, axis=0, keepdims=True) + EPS)
            normed = (values * scale * gain_ref[:, s : s + 1]).astype(BF)
            for tau in range(3):
                to = f + 1 - tau
                if 0 <= to < frames:
                    unfolded[
                        half, tau * width : (tau + 1) * width, to * LANES : (to + 1) * LANES
                    ] = normed
        pltpu.make_async_copy(taps_in[0], taps.at[s], sem_w.at[s, 0]).wait()
        pltpu.make_async_copy(rest_in[0], rest.at[s], sem_w.at[s, 1]).wait()
        film = 1.0 + transposed_dot(rest[s, width : width + 16], chosen)
        film = jnp.concatenate([film, film], axis=1)
        if s == 2:
            skip_load.wait()
        for j in range(frames // 2):
            cols = slice(2 * j * LANES, 2 * (j + 1) * LANES)
            mixed = transposed_dot(taps[s], unfolded[half, :, cols]) * film
            hidden = (mixed * (0.5 + 0.5 * jnp.tanh(0.5 * mixed))).astype(BF)
            total = pair(source, j).astype(F32) + transposed_dot(rest[s, 0:width], hidden)
            if s >= 2:
                total = total + transposed_dot(skip[s - 2], pair(one if s == 2 else first, j))
            total = total.astype(BF)
            if s == 3:
                last[2 * j] = total[:, :LANES]
                last[2 * j + 1] = total[:, LANES:]
            else:
                target[:, cols] = total
    stores = [pltpu.make_async_copy(last.at[me ^ d], outs[d], sem_o.at[d]) for d in range(frames)]
    for store in stores:
        store.start()
    for store in stores:
        store.wait()


def run_sections(blocks, taps, rest, skip, gain):
    frames = len(blocks)
    width = gain.shape[0]
    columns = frames * LANES
    anywhere = pl.BlockSpec(memory_space=pl.ANY)
    return pl.pallas_call(
        functools.partial(sections_kernel, frames, width),
        out_shape=[jax.ShapeDtypeStruct((width, LANES), BF)] * frames,
        in_specs=[anywhere] * (frames + 9) + [pl.BlockSpec(memory_space=pltpu.VMEM)],
        out_specs=[anywhere] * frames,
        scratch_shapes=[
            pltpu.VMEM((frames, width, LANES), BF),
            pltpu.VMEM((4, 3 * width, width), BF),
            pltpu.VMEM((4, width + 16, width), BF),
            pltpu.VMEM((2, width, width), BF),
            pltpu.VMEM((2, 3 * width, columns), BF),
            pltpu.VMEM((width, columns), BF),
            pltpu.VMEM((width, columns), BF),
            pltpu.VMEM((frames, width, LANES), BF),
            pltpu.SemaphoreType.DMA((frames,)),
            pltpu.SemaphoreType.DMA((4, 2)),
            pltpu.SemaphoreType.DMA,
            pltpu.SemaphoreType.DMA((frames,)),
        ],
        compiler_params=pltpu.CompilerParams(vmem_limit_bytes=40 << 20),
        name="sections",
    )(*blocks, *taps, *rest, skip, gain)


def join_kernel(frames, *refs):
    blocks, out, sems = refs[:frames], refs[frames], refs[frames + 1]
    me = lax.axis_index("frame")
    copies = []
    for d in range(frames):
        lane = pl.multiple_of((me ^ d) * LANES, LANES)
        copies.append(pltpu.make_async_copy(blocks[d], out.at[:, pl.ds(lane, LANES)], sems.at[d]))
    for copy in copies:
        copy.start()
    for copy in copies:
        copy.wait()


def join_blocks(blocks):
    frames = len(blocks)
    width = blocks[0].shape[0]
    return pl.pallas_call(
        functools.partial(join_kernel, frames),
        out_shape=jax.ShapeDtypeStruct((width, frames * LANES), BF),
        in_specs=[pl.BlockSpec(memory_space=pl.ANY)] * frames,
        out_specs=pl.BlockSpec(memory_space=pl.ANY),
        scratch_shapes=[pltpu.SemaphoreType.DMA((frames,))],
        name="join",
    )(*blocks)


def block_shards(clips, timesteps, gain, temporal_weight, film_weight, out_weight, skip_weight):
    frames = lax.axis_size("frame")
    width = clips.shape[2]
    own = clips[0, 0]
    me = lax.axis_index("frame")
    order = [6, 7, 4, 5, 2, 3, 1]

    taps0 = temporal_weight[0].reshape(3 * width, width)
    taps2 = exchange(taps0, "segment", 2)
    cut = [lax.dynamic_slice_in_dim(own, (me ^ d) * LANES, LANES, 1) for d in range(frames)]
    cut = lax.optimization_barrier(tuple(cut))
    got = {0: cut[0]}
    for d in order:
        got[d] = exchange(cut[d], "frame", d)

    film = jnp.dot(embed(timesteps, width), film_weight[0], preferred_element_type=F32)
    high = film.astype(BF)
    low = (film - high.astype(F32)).astype(BF)
    rest0 = jnp.concatenate([out_weight[0], high, low, jnp.zeros((8, width), BF)], axis=0)
    rest2 = exchange(rest0, "segment", 2)
    taps1 = exchange(taps0, "segment", 1)
    rest1 = exchange(rest0, "segment", 1)
    taps3 = exchange(taps2, "segment", 1)
    rest3 = exchange(rest2, "segment", 1)

    outs = run_sections(
        [got[d] for d in range(frames)],
        [taps0, taps1, taps2, taps3],
        [rest0, rest1, rest2, rest3],
        skip_weight,
        gain.T,
    )
    back = {0: outs[0]}
    for d in order:
        back[d] = exchange(outs[d], "frame", d)
    return join_blocks([back[d] for d in range(frames)])[None, None]


def solution(mesh):
    placed = (
        P("segment", "frame", None, None),
        P(),
        P(),
        P("segment", None, None, None),
        P("segment", None, None),
        P("segment", None, None),
        P(),
    )

    def run(*arrays):
        clips, gain = arrays[0], arrays[2]
        split = mesh.shape["frame"]
        fits = (
            clips.shape[1] == split
            and split & (split - 1) == 0
            and split == 8
            and clips.shape[3] == split * LANES
            and clips.shape[2] % 64 == 0
            and clips.shape[0] == gain.shape[0] == mesh.shape["segment"] == 4
        )
        return jax.shard_map(
            block_shards if fits else plain_shards,
            mesh=mesh,
            in_specs=placed,
            out_specs=P("segment", "frame", None, None),
            check_vma=False,
        )(*arrays)

    return run
```

```python
import functools
import math

import jax
import jax.numpy as jnp
from jax import lax
from jax.experimental import pallas as pl
from jax.experimental.pallas import tpu as pltpu
from jax.sharding import PartitionSpec as P

BF = jnp.bfloat16
F32 = jnp.float32
LANES = 128
EPS = 1e-05


def embed(timesteps, width):
    half = width // 2
    freq = jnp.exp(-math.log(10000.0) * jnp.arange(half, dtype=jnp.float32) / half)
    angle = timesteps.astype(jnp.float32)[:, None] * freq[None, :]
    return jnp.concatenate([jnp.sin(angle), jnp.cos(angle)], axis=-1).astype(jnp.bfloat16)


def exchange(array, axis, by):
    return lax.ppermute(array, axis, [(i, i ^ by) for i in range(lax.axis_size(axis))])


def plain_section(state, gain, taps, film, projection, extra):
    values = state.astype(F32)
    meansq = jnp.mean(values * values, axis=1, keepdims=True)
    normed = (values * lax.rsqrt(meansq + EPS) * gain[None, :, None]).astype(BF)
    padded = jnp.pad(normed, ((1, 1), (0, 0), (0, 0)))
    count = state.shape[0]
    mixed = sum(
        jnp.einsum("io,fip->fop", taps[tau], padded[tau : tau + count], preferred_element_type=F32)
        for tau in range(3)
    )
    hidden = jax.nn.silu(mixed * (1.0 + film[None, :, None])).astype(BF)
    total = values + jnp.einsum("io,fip->fop", projection, hidden, preferred_element_type=F32)
    if extra is not None:
        total = total + jnp.einsum("io,fip->fop", extra[0], extra[1], preferred_element_type=F32)
    return total.astype(BF)


def plain_shards(clips, timesteps, gain, temporal_weight, film_weight, out_weight, skip_weight):
    own = clips[0]
    pixels = own.shape[2]
    split = lax.axis_size("frame")
    pad = -pixels % split
    if pad:
        own = jnp.pad(own, ((0, 0), (0, 0), (0, pad)))
    state = lax.all_to_all(own, "frame", 2, 0, tiled=True)
    emb = embed(timesteps, clips.shape[2])
    film = jnp.dot(emb, film_weight[0], preferred_element_type=F32)
    taps = lax.all_gather(temporal_weight[0], "segment")
    projection = lax.all_gather(out_weight[0], "segment")
    films = lax.all_gather(film, "segment")
    micro = lax.axis_index("segment")
    first = state
    skips = {}
    for section in range(gain.shape[0]):
        extra = None
        if section == 2:
            extra = (skip_weight[0], skips[0])
        if section == 3:
            extra = (skip_weight[1], first)
        film_vec = lax.dynamic_index_in_dim(films[section], micro, 0, keepdims=False)
        state = plain_section(
            state, gain[section], taps[section], film_vec, projection[section], extra
        )
        skips[section] = state
    result = lax.all_to_all(state, "frame", 0, 2, tiled=True)
    return result[None, :, :, :pixels]


FILM_ROWS = 16


def place():
    segment, frame = lax.axis_index("segment"), lax.axis_index("frame")
    return segment // 2, segment % 2, frame // 2, frame % 2


def devices():
    for segment in range(4):
        for frame in range(8):
            yield segment, frame, (segment // 2, segment % 2, frame // 2, frame % 2)


def move(array, rule):
    pairs = []
    for segment, frame, (y, c, z, x) in devices():
        y, c, z, x = rule(y, c, z, x)
        pairs.append((segment * 8 + frame, (2 * y + c) * 8 + 2 * z + x))
    return lax.ppermute(array, ("segment", "frame"), pairs)


def turn(array, by):
    return move(array, lambda y, c, z, x: (y, x, z ^ by, c))


def swap_cores(array):
    return move(array, lambda y, c, z, x: (y, 1 - c, z, x))


def swap_planes(array):
    return move(array, lambda y, c, z, x: (1 - y, c, z, x))


def pin(arrays, space):
    return [pltpu.with_memory_space_constraint(a, space) for a in arrays]


def pack_kernel(levels, times_ref, x_ref, taps_ref, projection_ref, film_ref, *outs):
    width = projection_ref.shape[0]
    pack = outs[levels]
    held = jnp.concatenate(
        [taps_ref[...].reshape(3 * width, width).T, projection_ref[...].T], axis=1
    )
    lane = lax.broadcasted_iota(jnp.int32, (8, width), 1)
    row = lax.broadcasted_iota(jnp.int32, (8, width), 0)
    half = width // 2
    index = jnp.where(lane < half, lane, lane - half).astype(F32)
    freq = jnp.exp(-math.log(10000.0) * index / half)
    times = jnp.zeros((8, width), jnp.int32)
    for m in range(4):
        times = jnp.where(row == m, times_ref[m], times)
    angle = times.astype(F32) * freq
    emb = jnp.where(lane < half, jnp.sin(angle), jnp.cos(angle)).astype(BF)
    film = jnp.dot(emb, film_ref[...], preferred_element_type=F32)
    high = film.astype(BF).astype(F32)
    rows = jnp.concatenate([high[0:4], (film - high)[0:4], jnp.zeros((8, width), F32)], axis=0)
    rows = jnp.concatenate([rows.astype(BF), jnp.zeros((FILM_ROWS, 3 * width), BF)], axis=1)
    pack[0:width] = held
    pack[width:] = rows
    z = lax.axis_index("frame") // 2
    for d in range(levels):
        for k in range(2):
            at = pl.multiple_of(((z ^ d) * 2 + k) * LANES, LANES)
            outs[d][k] = x_ref[:, pl.ds(at, LANES)]


def pack_and_cut(times, own, taps, projection, film_weight, levels):
    width = own.shape[0]
    vmem = pl.BlockSpec(memory_space=pltpu.VMEM)
    return pl.pallas_call(
        functools.partial(pack_kernel, levels),
        out_shape=[jax.ShapeDtypeStruct((2, width, LANES), BF)] * levels
        + [jax.ShapeDtypeStruct((width + FILM_ROWS, 4 * width), BF)],
        in_specs=[pl.BlockSpec(memory_space=pltpu.SMEM)] + [vmem] * 4,
        out_specs=[vmem] * (levels + 1),
        name="pack",
    )(times, own, taps, projection, film_weight)


def join_kernel(levels, *refs):
    blocks, out = refs[:levels], refs[levels]
    frame = lax.axis_index("frame")
    z, x = frame // 2, frame % 2
    for d in range(levels):
        for k in range(2):
            at = pl.multiple_of(((z ^ d) * 2 + (x ^ k)) * LANES, LANES)
            out[:, pl.ds(at, LANES)] = blocks[d][k]


def join_blocks(blocks):
    levels, width = len(blocks), blocks[0].shape[1]
    vmem = pl.BlockSpec(memory_space=pltpu.VMEM)
    return pl.pallas_call(
        functools.partial(join_kernel, levels),
        out_shape=jax.ShapeDtypeStruct((width, 2 * levels * LANES), BF),
        in_specs=[vmem] * levels,
        out_specs=vmem,
        name="join",
    )(*pin(blocks, pltpu.VMEM))


def sections_kernel(spans, dests, borders, levels, width, loaded, *refs):
    refs = list(refs)

    def take(count):
        taken = refs[:count]
        del refs[:count]
        return taken

    near = borders is not None and spans[0][0] == 0
    turned, swapped = take(len(loaded)), take(len(loaded))
    packs = take(4)
    skip_in, gain_ref = take(2)
    if near:
        (border_in,) = take(1)
    kept, given = take(2)
    if borders and not near:
        (border_out,) = take(1)
    first, weights, skip, unfolded, with_one, with_first, two, three, last, bordering = take(10)
    sem_x, sem_w, sem_s, sem_o, sem_b = take(5)
    y, core, z, x = place()
    clip = 2 * y + x
    segment = 2 * y + core
    frames = 2 * levels
    upper = jnp.where(z >= levels // 2, 1, 0)
    mirror = upper * (frames - 1)

    loads = []
    for n, d in enumerate(loaded):
        for k in range(2):
            slot = (2 * (z ^ d) + (core ^ k)) ^ mirror
            source = (turned, swapped)[k][n].at[core]
            loads.append(pltpu.make_async_copy(source, first.at[slot], sem_x.at[2 * n + k]))
    if near:
        loads.append(pltpu.make_async_copy(border_in, bordering, sem_b))
    for load in loads:
        load.start()

    for s in range(4):
        for b in range(4):

            @pl.when(segment ^ s == b)
            def _():
                pltpu.make_async_copy(packs[b], weights.at[s], sem_w.at[s]).start()

    skip_load = pltpu.make_async_copy(skip_in, skip, sem_s)
    skip_load.start()

    def rows_of(step):
        return pl.ds(pl.multiple_of((1 - step + 2 * step * upper) * width, 64), width)

    def span(f, count=1):
        return slice(f * LANES, (f + count) * LANES)

    zeros = jnp.zeros((width, LANES), BF)
    unfolded[3 * width :, :] = jnp.zeros((unfolded.shape[0] - 3 * width, frames * LANES), BF)
    unfolded[rows_of(1), span(0)] = zeros
    unfolded[rows_of(-1), span(frames - 1)] = zeros
    for ref in (with_one, with_first):
        ref[0:64, :] = jnp.zeros((64, frames * LANES), BF)

    def column_of(rows, chosen):
        at = lax.broadcasted_iota(jnp.int32, (16, LANES), 0)
        hit = functools.reduce(jnp.logical_or, [at == c for c in chosen])
        return lax.dot_general(
            rows,
            jnp.where(hit, 1.0, 0.0).astype(BF),
            (((0,), (0,)), ((), ())),
            preferred_element_type=F32,
        )

    gains = []
    rest = gain_ref[...]
    for _ in range(3):
        gains.append(rest.astype(BF).astype(F32))
        rest = rest - gains[-1]
    gains = jnp.concatenate(gains + [jnp.zeros_like(rest)], axis=0).astype(BF)

    for load in loads:
        load.wait()
    one, zero = with_one.at[64 + width :, :], with_first.at[64 + width :, :]
    states = (zero, one, two, three)
    for f in range(2 * len(loaded)):
        zero[:, span(f)] = first[f]
    if near:
        for n, (s, f) in enumerate(borders):
            states[s][:, span(f)] = bordering[n]

    for s, (low, high) in enumerate(spans):
        source = states[s]
        gain = column_of(gains, [s, 4 + s, 8 + s])
        for f in range(max(low - 1, 0), min(high + 1, frames)):
            values = source[:, span(f)].astype(F32)
            scale = lax.rsqrt(jnp.mean(values * values, axis=0, keepdims=True) + EPS)
            normed = (values * scale * gain).astype(BF)
            for step in (-1, 0, 1):
                if low <= f + step < high:
                    unfolded[rows_of(step), span(f + step)] = normed
        pltpu.make_async_copy(packs[0], weights.at[s], sem_w.at[s]).wait()
        film = 1.0 + column_of(weights[s, width:, 0:width], [clip, 4 + clip])
        film = jnp.concatenate([film] * (high - low), axis=1)
        cols = span(low, high - low)
        taps = weights[s, 0:width, 0 : unfolded.shape[0]]
        mixed = jnp.dot(taps, unfolded[:, cols], preferred_element_type=F32) * film
        hidden = (mixed * (0.5 + 0.5 * jnp.tanh(0.5 * mixed))).astype(BF)
        projection = weights[s, 0:width, 3 * width - 64 :]
        if s < 2:
            with_one[64 : 64 + width, cols] = hidden
            right = with_one[0 : 64 + width, cols]
        else:
            if s == 2:
                skip_load.wait()
            beside = with_one if s == 2 else with_first
            beside[64 : 64 + width, cols] = hidden
            right = beside[:, cols]
            projection = jnp.concatenate([projection, skip[s - 2].T], axis=1)
        total = source[:, cols].astype(F32)
        total = (total + jnp.dot(projection, right, preferred_element_type=F32)).astype(BF)
        if s < 3:
            states[s + 1][:, cols] = total
        else:
            for f in range(low, high):
                last[f] = total[:, span(f - low)]
    stores = []
    for n, d in enumerate(dests):
        for k, out in enumerate((kept, given)):
            slot = (2 * (z ^ d) + (core ^ k)) ^ mirror
            stores.append(
                pltpu.make_async_copy(last.at[slot], out.at[n], sem_o.at[2 * n + k])
            )
    if borders and not near:
        for n, (s, f) in enumerate(borders):
            bordering[n] = states[s][:, span(f)]
        stores.append(pltpu.make_async_copy(bordering, border_out, sem_b))
    for store in stores:
        store.start()
    for store in stores:
        store.wait()


def run_sections(spans, dests, borders, turned, swapped, weights, skip, gain, border=None):
    levels = lax.axis_size("frame") // 2
    frames = 2 * levels
    width = gain.shape[1]
    columns = frames * LANES
    hbm = pl.BlockSpec(memory_space=pltpu.HBM)
    vmem = pl.BlockSpec(memory_space=pltpu.VMEM)
    given_out = [jax.ShapeDtypeStruct((len(dests), width, LANES), BF)] * 2
    blocks, inputs = [*turned, *swapped], [*weights, skip]
    after = []
    if border is not None:
        after = pin([border], pltpu.HBM)
    elif borders:
        given_out.append(jax.ShapeDtypeStruct((len(borders), width, LANES), BF))
    flops = sum(high - low for low, high in spans) * LANES * 2 * 5 * width * width
    return pl.pallas_call(
        functools.partial(
            sections_kernel, spans, dests, borders, levels, width, list(range(len(turned)))
        ),
        out_shape=given_out,
        in_specs=[vmem] * len(blocks)
        + [hbm] * len(inputs)
        + [pl.BlockSpec(memory_space=pltpu.VMEM)]
        + [hbm] * len(after),
        out_specs=[hbm] * len(given_out),
        scratch_shapes=[
            pltpu.VMEM((frames, width, LANES), BF),
            pltpu.VMEM((4, width + FILM_ROWS, 4 * width), BF),
            pltpu.VMEM((2, width, width), BF),
            pltpu.VMEM((3 * width + 64, columns), BF),
            pltpu.VMEM((2 * width + 64, columns), BF),
            pltpu.VMEM((2 * width + 64, columns), BF),
            pltpu.VMEM((width, columns), BF),
            pltpu.VMEM((width, columns), BF),
            pltpu.VMEM((frames, width, LANES), BF),
            pltpu.VMEM((6, width, LANES), BF),
            pltpu.SemaphoreType.DMA((frames,)),
            pltpu.SemaphoreType.DMA((4,)),
            pltpu.SemaphoreType.DMA,
            pltpu.SemaphoreType.DMA((frames,)),
            pltpu.SemaphoreType.DMA,
        ],
        compiler_params=pltpu.CompilerParams(vmem_limit_bytes=40 << 20),
        cost_estimate=pl.CostEstimate(flops=flops, bytes_accessed=4 << 20, transcendentals=0),
        name="sections",
    )(*pin(blocks, pltpu.VMEM), *pin(inputs, pltpu.HBM), gain, *after)


def send_back(kept, given, dests):
    swapped = swap_cores(given)
    blocks = [jnp.stack([kept[n], swapped[n]]) for n in range(len(dests))]
    return [turn(block, d) for block, d in zip(blocks, dests, strict=True)], blocks


SPLIT = False


def block_shards(clips, timesteps, gain, temporal_weight, film_weight, out_weight, skip_weight):
    levels = lax.axis_size("frame") // 2
    order = [3, 2, 1, 0]

    *cut, pack0 = pack_and_cut(
        timesteps, clips[0, 0], temporal_weight[0], out_weight[0], film_weight[0], levels
    )
    pack2 = swap_planes(pack0)
    turned = [None] * levels
    for d in order:
        turned[d] = turn(cut[d], d)
    pack1 = swap_cores(pack0)

    turned, pack2 = lax.optimization_barrier((turned, pack2))
    swapped = [swap_cores(block) for block in turned]
    pack3 = swap_cores(pack2)

    weights = [pack0, pack1, pack2, pack3]
    frames = 2 * levels
    if SPLIT:
        borders = [(1, 1), (1, 2), (2, 2), (2, 3), (3, 3), (3, 4)]
        far = [(s + 1, frames) for s in range(4)]
        kept, given, border = run_sections(
            far, [2, 3], borders, turned, swapped, weights, skip_weight, gain
        )
        back, blocks = send_back(kept, given, [2, 3])
        border, _ = lax.optimization_barrier((border, blocks))
        kept, given = run_sections(
            [(0, s + 1) for s in range(4)],
            [0, 1],
            borders,
            turned[:2],
            swapped[:2],
            weights,
            skip_weight,
            gain,
            border,
        )
        back = send_back(kept, given, [0, 1])[0] + back
    else:
        kept, given = run_sections(
            [(0, frames)] * 4, [0, 1, 2, 3], None, turned, swapped, weights, skip_weight, gain
        )
        back = send_back(kept, given, [0, 1, 2, 3])[0]
    return join_blocks(back)[None, None]


def solution(mesh):
    placed = (
        P("segment", "frame", None, None),
        P(),
        P(),
        P("segment", None, None, None),
        P("segment", None, None),
        P("segment", None, None),
        P(),
    )

    def run(*arrays):
        clips, gain = arrays[0], arrays[2]
        split = mesh.shape["frame"]
        fits = (
            clips.shape[1] == split == 8
            and clips.shape[3] == split * LANES
            and clips.shape[2] % 64 == 0
            and clips.shape[0] == gain.shape[0] == mesh.shape["segment"] == 4
        )
        return jax.shard_map(
            block_shards if fits else plain_shards,
            mesh=mesh,
            in_specs=placed,
            out_specs=P("segment", "frame", None, None),
            check_vma=False,
        )(*arrays)

    return run
```

```python
import functools
import math

import jax
import jax.numpy as jnp
from jax import lax
from jax.experimental import pallas as pl
from jax.experimental.pallas import tpu as pltpu
from jax.sharding import PartitionSpec as P

BF = jnp.bfloat16
F32 = jnp.float32
LANES = 128
EPS = 1e-05


def embed(timesteps, width):
    half = width // 2
    freq = jnp.exp(-math.log(10000.0) * jnp.arange(half, dtype=jnp.float32) / half)
    angle = timesteps.astype(jnp.float32)[:, None] * freq[None, :]
    return jnp.concatenate([jnp.sin(angle), jnp.cos(angle)], axis=-1).astype(jnp.bfloat16)


def exchange(array, axis, by):
    return lax.ppermute(array, axis, [(i, i ^ by) for i in range(lax.axis_size(axis))])


def plain_section(state, gain, taps, film, projection, extra):
    values = state.astype(F32)
    meansq = jnp.mean(values * values, axis=1, keepdims=True)
    normed = (values * lax.rsqrt(meansq + EPS) * gain[None, :, None]).astype(BF)
    padded = jnp.pad(normed, ((1, 1), (0, 0), (0, 0)))
    count = state.shape[0]
    mixed = sum(
        jnp.einsum("io,fip->fop", taps[tau], padded[tau : tau + count], preferred_element_type=F32)
        for tau in range(3)
    )
    hidden = jax.nn.silu(mixed * (1.0 + film[None, :, None])).astype(BF)
    total = values + jnp.einsum("io,fip->fop", projection, hidden, preferred_element_type=F32)
    if extra is not None:
        total = total + jnp.einsum("io,fip->fop", extra[0], extra[1], preferred_element_type=F32)
    return total.astype(BF)


def plain_shards(clips, timesteps, gain, temporal_weight, film_weight, out_weight, skip_weight):
    own = clips[0]
    pixels = own.shape[2]
    split = lax.axis_size("frame")
    pad = -pixels % split
    if pad:
        own = jnp.pad(own, ((0, 0), (0, 0), (0, pad)))
    state = lax.all_to_all(own, "frame", 2, 0, tiled=True)
    emb = embed(timesteps, clips.shape[2])
    film = jnp.dot(emb, film_weight[0], preferred_element_type=F32)
    taps = lax.all_gather(temporal_weight[0], "segment")
    projection = lax.all_gather(out_weight[0], "segment")
    films = lax.all_gather(film, "segment")
    micro = lax.axis_index("segment")
    first = state
    skips = {}
    for section in range(gain.shape[0]):
        extra = None
        if section == 2:
            extra = (skip_weight[0], skips[0])
        if section == 3:
            extra = (skip_weight[1], first)
        film_vec = lax.dynamic_index_in_dim(films[section], micro, 0, keepdims=False)
        state = plain_section(
            state, gain[section], taps[section], film_vec, projection[section], extra
        )
        skips[section] = state
    result = lax.all_to_all(state, "frame", 0, 2, tiled=True)
    return result[None, :, :, :pixels]


FILM_ROWS = 16


def place():
    segment, frame = lax.axis_index("segment"), lax.axis_index("frame")
    return segment // 2, segment % 2, frame // 2, frame % 2


def devices():
    for segment in range(4):
        for frame in range(8):
            yield segment, frame, (segment // 2, segment % 2, frame // 2, frame % 2)


def move(array, rule):
    pairs = []
    for segment, frame, (y, c, z, x) in devices():
        y, c, z, x = rule(y, c, z, x)
        pairs.append((segment * 8 + frame, (2 * y + c) * 8 + 2 * z + x))
    return lax.ppermute(array, ("segment", "frame"), pairs)


def turn(array, by):
    return move(array, lambda y, c, z, x: (y, x, z ^ by, c))


def swap_cores(array):
    return move(array, lambda y, c, z, x: (y, 1 - c, z, x))


def swap_planes(array):
    return move(array, lambda y, c, z, x: (1 - y, c, z, x))


def pin(arrays, space):
    return [pltpu.with_memory_space_constraint(a, space) for a in arrays]


def pack_kernel(levels, times_ref, x_ref, taps_ref, projection_ref, film_ref, *outs):
    width = projection_ref.shape[0]
    pack = outs[levels]
    held = jnp.concatenate(
        [taps_ref[...].reshape(3 * width, width).T, projection_ref[...].T], axis=1
    )
    lane = lax.broadcasted_iota(jnp.int32, (8, width), 1)
    row = lax.broadcasted_iota(jnp.int32, (8, width), 0)
    half = width // 2
    index = jnp.where(lane < half, lane, lane - half).astype(F32)
    freq = jnp.exp(-math.log(10000.0) * index / half)
    times = jnp.zeros((8, width), jnp.int32)
    for m in range(4):
        times = jnp.where(row == m, times_ref[m], times)
    angle = times.astype(F32) * freq
    emb = jnp.where(lane < half, jnp.sin(angle), jnp.cos(angle)).astype(BF)
    film = jnp.dot(emb, film_ref[...], preferred_element_type=F32)
    high = film.astype(BF).astype(F32)
    rows = jnp.concatenate([high[0:4], (film - high)[0:4], jnp.zeros((8, width), F32)], axis=0)
    rows = jnp.concatenate([rows.astype(BF), jnp.zeros((FILM_ROWS, 3 * width), BF)], axis=1)
    pack[0:width] = held
    pack[width:] = rows
    z = lax.axis_index("frame") // 2
    for d in range(levels):
        for k in range(2):
            at = pl.multiple_of(((z ^ d) * 2 + k) * LANES, LANES)
            outs[d][k] = x_ref[:, pl.ds(at, LANES)]


def pack_and_cut(times, own, taps, projection, film_weight, levels):
    width = own.shape[0]
    vmem = pl.BlockSpec(memory_space=pltpu.VMEM)
    return pl.pallas_call(
        functools.partial(pack_kernel, levels),
        out_shape=[jax.ShapeDtypeStruct((2, width, LANES), BF)] * levels
        + [jax.ShapeDtypeStruct((width + FILM_ROWS, 4 * width), BF)],
        in_specs=[pl.BlockSpec(memory_space=pltpu.SMEM)] + [vmem] * 4,
        out_specs=[vmem] * (levels + 1),
        name="pack",
    )(times, own, taps, projection, film_weight)


def join_kernel(order, *refs):
    blocks, out = refs[: len(order)], refs[len(order)]
    frame = lax.axis_index("frame")
    z, x = frame // 2, frame % 2
    for n, d in enumerate(order):
        for k in range(2):
            at = pl.multiple_of(((z ^ d) * 2 + (x ^ k)) * LANES, LANES)
            out[:, pl.ds(at, LANES)] = blocks[n][k]


def join_blocks(blocks, order):
    levels, width = len(blocks), blocks[0].shape[1]
    vmem = pl.BlockSpec(memory_space=pltpu.VMEM)
    return pl.pallas_call(
        functools.partial(join_kernel, order),
        out_shape=jax.ShapeDtypeStruct((width, 2 * levels * LANES), BF),
        in_specs=[vmem] * levels,
        out_specs=vmem,
        name="join",
    )(*pin(blocks, pltpu.VMEM))


def sections_kernel(spans, dests, borders, levels, width, loaded, *refs):
    refs = list(refs)

    def take(count):
        taken = refs[:count]
        del refs[:count]
        return taken

    near = borders is not None and spans[0][0] == 0
    turned, swapped = take(len(loaded)), take(len(loaded))
    packs = take(4)
    skip_in, gain_ref = take(2)
    if near:
        (border_in,) = take(1)
    kept, given = take(2)
    if borders and not near:
        (border_out,) = take(1)
    weights, skip, unfolded, with_one, with_first, two, three, last, bordering = take(9)
    sem_w, sem_s, sem_b = take(3)
    y, core, z, x = place()
    clip = 2 * y + x
    segment = 2 * y + core
    frames = 2 * levels
    upper = jnp.where(z >= levels // 2, 1, 0)
    mirror = upper * (frames - 1)

    def load_weights(s):
        for b in range(4):

            @pl.when(segment ^ s == b)
            def _():
                pltpu.make_async_copy(packs[b], weights.at[s], sem_w.at[s]).start()

    load_weights(0)
    if near:
        border_load = pltpu.make_async_copy(border_in, bordering, sem_b)
        border_load.start()
    skip_load = pltpu.make_async_copy(skip_in, skip, sem_s)

    def rows_of(step):
        return pl.ds(pl.multiple_of((1 - step + 2 * step * upper) * width, 64), width)

    def lanes_of(d, k):
        slot = (2 * (z ^ d) + (core ^ k)) ^ mirror
        return pl.ds(pl.multiple_of(slot * LANES, LANES), LANES)

    def span(f, count=1):
        return slice(f * LANES, (f + count) * LANES)

    zeros = jnp.zeros((width, LANES), BF)
    unfolded[3 * width :, :] = jnp.zeros((unfolded.shape[0] - 3 * width, frames * LANES), BF)
    unfolded[rows_of(1), span(0)] = zeros
    unfolded[rows_of(-1), span(frames - 1)] = zeros
    for ref in (with_one, with_first):
        ref[0:64, :] = jnp.zeros((64, frames * LANES), BF)

    def column_of(rows, chosen):
        at = lax.broadcasted_iota(jnp.int32, (16, LANES), 0)
        hit = functools.reduce(jnp.logical_or, [at == c for c in chosen])
        return lax.dot_general(
            rows,
            jnp.where(hit, 1.0, 0.0).astype(BF),
            (((0,), (0,)), ((), ())),
            preferred_element_type=F32,
        )

    gains = []
    rest = gain_ref[...]
    for _ in range(3):
        gains.append(rest.astype(BF).astype(F32))
        rest = rest - gains[-1]
    gains = jnp.concatenate(gains + [jnp.zeros_like(rest)], axis=0).astype(BF)

    one, zero = with_one.at[64 + width :, :], with_first.at[64 + width :, :]
    states = (zero, one, two, three)
    for n, d in enumerate(loaded):
        for k in range(2):
            zero[:, lanes_of(d, k)] = (turned, swapped)[k][n][core]
    if near:
        border_load.wait()
        for n, (s, f) in enumerate(borders):
            states[s][:, span(f)] = bordering[n]

    for s, (low, high) in enumerate(spans):
        source = states[s]
        gain = column_of(gains, [s, 4 + s, 8 + s])
        for f in range(max(low - 1, 0), min(high + 1, frames)):
            values = source[:, span(f)].astype(F32)
            scale = lax.rsqrt(jnp.mean(values * values, axis=0, keepdims=True) + EPS)
            normed = (values * scale * gain).astype(BF)
            for step in (-1, 0, 1):
                if low <= f + step < high:
                    unfolded[rows_of(step), span(f + step)] = normed
        pltpu.make_async_copy(packs[0], weights.at[s], sem_w.at[s]).wait()
        if s < 3:
            load_weights(s + 1)
        if s == 0:
            skip_load.start()
        film = 1.0 + column_of(weights[s, width:, 0:width], [clip, 4 + clip])
        film = jnp.concatenate([film] * (high - low), axis=1)
        cols = span(low, high - low)
        taps = weights[s, 0:width, 0 : unfolded.shape[0]]
        mixed = jnp.dot(taps, unfolded[:, cols], preferred_element_type=F32) * film
        hidden = (mixed * (0.5 + 0.5 * jnp.tanh(0.5 * mixed))).astype(BF)
        projection = weights[s, 0:width, 3 * width - 64 :]
        if s < 2:
            with_one[64 : 64 + width, cols] = hidden
            right = with_one[0 : 64 + width, cols]
        else:
            if s == 2:
                skip_load.wait()
            beside = with_one if s == 2 else with_first
            beside[64 : 64 + width, cols] = hidden
            right = beside[:, cols]
            projection = jnp.concatenate([projection, skip[s - 2].T], axis=1)
        total = source[:, cols].astype(F32)
        total = (total + jnp.dot(projection, right, preferred_element_type=F32)).astype(BF)
        (one, two, three, last)[s][:, cols] = total
    for n, d in enumerate(dests):
        for k, out in enumerate((kept, given)):
            out[n] = last[:, lanes_of(d, k)]
    if borders and not near:
        for n, (s, f) in enumerate(borders):
            border_out[n] = states[s][:, span(f)]


def run_sections(
    spans, dests, borders, loaded, turned, swapped, weights, skip, gain, border=None
):
    levels = lax.axis_size("frame") // 2
    frames = 2 * levels
    width = gain.shape[1]
    columns = frames * LANES
    hbm = pl.BlockSpec(memory_space=pltpu.HBM)
    vmem = pl.BlockSpec(memory_space=pltpu.VMEM)
    given_out = [pltpu.VMEM((len(dests), width, LANES), BF)] * 2
    blocks = [*turned, *swapped]
    inputs = [*pin(weights[:3], pltpu.HBM), *pin(weights[3:], pltpu.VMEM), *pin([skip], pltpu.HBM)]
    after = []
    if border is not None:
        after = pin([border], pltpu.HBM)
    elif borders:
        given_out.append(jax.ShapeDtypeStruct((len(borders), width, LANES), BF))
    flops = sum(high - low for low, high in spans) * LANES * 2 * 5 * width * width
    return pl.pallas_call(
        functools.partial(
            sections_kernel, spans, dests, borders, levels, width, loaded
        ),
        out_shape=given_out,
        in_specs=[vmem] * len(blocks)
        + [hbm] * 3
        + [vmem, hbm]
        + [pl.BlockSpec(memory_space=pltpu.VMEM)]
        + [hbm] * len(after),
        out_specs=[vmem] * len(given_out),
        scratch_shapes=[
            pltpu.VMEM((4, width + FILM_ROWS, 4 * width), BF),
            pltpu.VMEM((2, width, width), BF),
            pltpu.VMEM((3 * width + 64, columns), BF),
            pltpu.VMEM((2 * width + 64, columns), BF),
            pltpu.VMEM((2 * width + 64, columns), BF),
            pltpu.VMEM((width, columns), BF),
            pltpu.VMEM((width, columns), BF),
            pltpu.VMEM((width, columns), BF),
            pltpu.VMEM((6, width, LANES), BF),
            pltpu.SemaphoreType.DMA((4,)),
            pltpu.SemaphoreType.DMA,
            pltpu.SemaphoreType.DMA,
        ],
        compiler_params=pltpu.CompilerParams(vmem_limit_bytes=40 << 20),
        cost_estimate=pl.CostEstimate(flops=flops, bytes_accessed=4 << 20, transcendentals=0),
        name="sections",
    )(*pin(blocks, pltpu.VMEM), *inputs, gain, *after)


IN_ORDER = (2, 3, 1, 0)
OUT_ORDER = (2, 3, 1, 0)


def block_shards(clips, timesteps, gain, temporal_weight, film_weight, out_weight, skip_weight):
    levels = lax.axis_size("frame") // 2

    *cut, pack0 = pack_and_cut(
        timesteps, clips[0, 0], temporal_weight[0], out_weight[0], film_weight[0], levels
    )
    pack2 = swap_planes(pack0)
    turned = [turn(cut[d], d) for d in IN_ORDER]
    pack1 = swap_cores(pack0)
    pack2, *turned = lax.optimization_barrier((pack2, *turned))
    pack3 = swap_cores(pack2)
    swapped = [swap_cores(block) for block in turned]

    kept, given = run_sections(
        [(0, 2 * levels)] * 4,
        OUT_ORDER,
        None,
        IN_ORDER,
        turned,
        swapped,
        [pack0, pack1, pack2, pack3],
        skip_weight,
        gain,
    )
    swapped = swap_cores(given)
    blocks = [jnp.stack([kept[n], swapped[n]]) for n in range(levels)]
    back = [turn(block, d) for block, d in zip(blocks, OUT_ORDER, strict=True)]
    return join_blocks(back, OUT_ORDER)[None, None]


def solution(mesh):
    placed = (
        P("segment", "frame", None, None),
        P(),
        P(),
        P("segment", None, None, None),
        P("segment", None, None),
        P("segment", None, None),
        P(),
    )

    def run(*arrays):
        clips, gain = arrays[0], arrays[2]
        split = mesh.shape["frame"]
        fits = (
            clips.shape[1] == split == 8
            and clips.shape[3] == split * LANES
            and clips.shape[2] % 64 == 0
            and clips.shape[0] == gain.shape[0] == mesh.shape["segment"] == 4
        )
        return jax.shard_map(
            block_shards if fits else plain_shards,
            mesh=mesh,
            in_specs=placed,
            out_specs=P("segment", "frame", None, None),
            check_vma=False,
        )(*arrays)

    return run
```

```python
import functools
import math

import jax
import jax.numpy as jnp
from jax import lax
from jax.experimental import pallas as pl
from jax.experimental.pallas import tpu as pltpu
from jax.sharding import PartitionSpec as P

BF = jnp.bfloat16
F32 = jnp.float32
LANES = 128
EPS = 1e-05


def embed(timesteps, width):
    half = width // 2
    freq = jnp.exp(-math.log(10000.0) * jnp.arange(half, dtype=jnp.float32) / half)
    angle = timesteps.astype(jnp.float32)[:, None] * freq[None, :]
    return jnp.concatenate([jnp.sin(angle), jnp.cos(angle)], axis=-1).astype(jnp.bfloat16)


def exchange(array, axis, by):
    return lax.ppermute(array, axis, [(i, i ^ by) for i in range(lax.axis_size(axis))])


def plain_section(state, gain, taps, film, projection, extra):
    values = state.astype(F32)
    meansq = jnp.mean(values * values, axis=1, keepdims=True)
    normed = (values * lax.rsqrt(meansq + EPS) * gain[None, :, None]).astype(BF)
    padded = jnp.pad(normed, ((1, 1), (0, 0), (0, 0)))
    count = state.shape[0]
    mixed = sum(
        jnp.einsum("io,fip->fop", taps[tau], padded[tau : tau + count], preferred_element_type=F32)
        for tau in range(3)
    )
    hidden = jax.nn.silu(mixed * (1.0 + film[None, :, None])).astype(BF)
    total = values + jnp.einsum("io,fip->fop", projection, hidden, preferred_element_type=F32)
    if extra is not None:
        total = total + jnp.einsum("io,fip->fop", extra[0], extra[1], preferred_element_type=F32)
    return total.astype(BF)


def plain_shards(clips, timesteps, gain, temporal_weight, film_weight, out_weight, skip_weight):
    own = clips[0]
    pixels = own.shape[2]
    split = lax.axis_size("frame")
    pad = -pixels % split
    if pad:
        own = jnp.pad(own, ((0, 0), (0, 0), (0, pad)))
    state = lax.all_to_all(own, "frame", 2, 0, tiled=True)
    emb = embed(timesteps, clips.shape[2])
    film = jnp.dot(emb, film_weight[0], preferred_element_type=F32)
    taps = lax.all_gather(temporal_weight[0], "segment")
    projection = lax.all_gather(out_weight[0], "segment")
    films = lax.all_gather(film, "segment")
    micro = lax.axis_index("segment")
    first = state
    skips = {}
    for section in range(gain.shape[0]):
        extra = None
        if section == 2:
            extra = (skip_weight[0], skips[0])
        if section == 3:
            extra = (skip_weight[1], first)
        film_vec = lax.dynamic_index_in_dim(films[section], micro, 0, keepdims=False)
        state = plain_section(
            state, gain[section], taps[section], film_vec, projection[section], extra
        )
        skips[section] = state
    result = lax.all_to_all(state, "frame", 0, 2, tiled=True)
    return result[None, :, :, :pixels]


FILM_ROWS = 16


def place():
    segment, frame = lax.axis_index("segment"), lax.axis_index("frame")
    return segment // 2, segment % 2, frame // 2, frame % 2


def devices():
    for segment in range(4):
        for frame in range(8):
            yield segment, frame, (segment // 2, segment % 2, frame // 2, frame % 2)


def move(array, rule):
    pairs = []
    for segment, frame, (y, c, z, x) in devices():
        y, c, z, x = rule(y, c, z, x)
        pairs.append((segment * 8 + frame, (2 * y + c) * 8 + 2 * z + x))
    return lax.ppermute(array, ("segment", "frame"), pairs)


def turn(array, by):
    return move(array, lambda y, c, z, x: (y, x, z ^ by, c))


def swap_cores(array):
    return move(array, lambda y, c, z, x: (y, 1 - c, z, x))


def swap_planes(array):
    return move(array, lambda y, c, z, x: (1 - y, c, z, x))


def pin(arrays, space):
    return [pltpu.with_memory_space_constraint(a, space) for a in arrays]


def pack_kernel(levels, times_ref, x_ref, taps_ref, projection_ref, film_ref, *outs):
    width = projection_ref.shape[0]
    pack = outs[levels]
    held = jnp.concatenate(
        [taps_ref[...].reshape(3 * width, width).T, projection_ref[...].T], axis=1
    )
    lane = lax.broadcasted_iota(jnp.int32, (8, width), 1)
    row = lax.broadcasted_iota(jnp.int32, (8, width), 0)
    half = width // 2
    index = jnp.where(lane < half, lane, lane - half).astype(F32)
    freq = jnp.exp(-math.log(10000.0) * index / half)
    times = jnp.zeros((8, width), jnp.int32)
    for m in range(4):
        times = jnp.where(row == m, times_ref[m], times)
    angle = times.astype(F32) * freq
    emb = jnp.where(lane < half, jnp.sin(angle), jnp.cos(angle)).astype(BF)
    film = jnp.dot(emb, film_ref[...], preferred_element_type=F32)
    high = film.astype(BF).astype(F32)
    rows = jnp.concatenate([high[0:4], (film - high)[0:4], jnp.zeros((8, width), F32)], axis=0)
    rows = jnp.concatenate([rows.astype(BF), jnp.zeros((FILM_ROWS, 3 * width), BF)], axis=1)
    pack[0:width] = held
    pack[width:] = rows
    z = lax.axis_index("frame") // 2
    for d in range(levels):
        for k in range(2):
            at = pl.multiple_of(((z ^ d) * 2 + k) * LANES, LANES)
            outs[d][k] = x_ref[:, pl.ds(at, LANES)]


def pack_and_cut(times, own, taps, projection, film_weight, levels):
    width = own.shape[0]
    vmem = pl.BlockSpec(memory_space=pltpu.VMEM)
    return pl.pallas_call(
        functools.partial(pack_kernel, levels),
        out_shape=[pltpu.VMEM((2, width, LANES), BF)] * levels
        + [pltpu.VMEM((width + FILM_ROWS, 4 * width), BF)],
        in_specs=[pl.BlockSpec(memory_space=pltpu.SMEM)] + [vmem] * 4,
        out_specs=[vmem] * (levels + 1),
        name="pack",
    )(times, own, taps, projection, film_weight)


def join_kernel(parts, *refs):
    blocks, out = refs[: len(parts)], refs[len(parts)]
    frame = lax.axis_index("frame")
    z, x = frame // 2, frame % 2
    for block, (d, halves) in zip(blocks, parts, strict=True):
        for n, k in enumerate(halves):
            at = pl.multiple_of(((z ^ d) * 2 + (x ^ k)) * LANES, LANES)
            out[:, pl.ds(at, LANES)] = block[n]


def join_blocks(blocks, parts):
    width = blocks[0].shape[1]
    columns = sum(len(halves) for _, halves in parts) * LANES
    vmem = pl.BlockSpec(memory_space=pltpu.VMEM)
    return pl.pallas_call(
        functools.partial(join_kernel, parts),
        out_shape=jax.ShapeDtypeStruct((width, columns), BF),
        in_specs=[vmem] * len(blocks),
        out_specs=vmem,
        name="join",
    )(*pin(blocks, pltpu.VMEM))


def sections_kernel(spans, dests, borders, levels, width, loaded, *refs):
    refs = list(refs)

    def take(count):
        taken = refs[:count]
        del refs[:count]
        return taken

    near = borders is not None and spans[0][0] == 0
    turned, swapped = take(len(loaded)), take(len(loaded))
    packs = take(4)
    skip_in, gain_ref = take(2)
    if near:
        (border_in,) = take(1)
    kept, given = take(2)
    if borders and not near:
        (border_out,) = take(1)
    weights, skip, unfolded, with_one, with_first, two, three, last, bordering = take(9)
    sem_w, sem_s, sem_b = take(3)
    y, core, z, x = place()
    clip = 2 * y + x
    segment = 2 * y + core
    frames = 2 * levels
    upper = jnp.where(z >= levels // 2, 1, 0)
    mirror = upper * (frames - 1)

    def load_weights(s):
        for b in range(4):

            @pl.when(segment ^ s == b)
            def _():
                pltpu.make_async_copy(packs[b], weights.at[s], sem_w.at[s]).start()

    load_weights(0)
    if near:
        border_load = pltpu.make_async_copy(border_in, bordering, sem_b)
        border_load.start()
    skip_load = pltpu.make_async_copy(skip_in, skip, sem_s)

    def rows_of(step):
        return pl.ds(pl.multiple_of((1 - step + 2 * step * upper) * width, 64), width)

    def lanes_of(d, k):
        slot = (2 * (z ^ d) + (core ^ k)) ^ mirror
        return pl.ds(pl.multiple_of(slot * LANES, LANES), LANES)

    def span(f, count=1):
        return slice(f * LANES, (f + count) * LANES)

    zeros = jnp.zeros((width, LANES), BF)
    unfolded[3 * width :, :] = jnp.zeros((unfolded.shape[0] - 3 * width, frames * LANES), BF)
    unfolded[rows_of(1), span(0)] = zeros
    unfolded[rows_of(-1), span(frames - 1)] = zeros
    for ref in (with_one, with_first):
        ref[0:64, :] = jnp.zeros((64, frames * LANES), BF)

    def column_of(rows, chosen):
        at = lax.broadcasted_iota(jnp.int32, (16, LANES), 0)
        hit = functools.reduce(jnp.logical_or, [at == c for c in chosen])
        return lax.dot_general(
            rows,
            jnp.where(hit, 1.0, 0.0).astype(BF),
            (((0,), (0,)), ((), ())),
            preferred_element_type=F32,
        )

    gains = []
    rest = gain_ref[...]
    for _ in range(3):
        gains.append(rest.astype(BF).astype(F32))
        rest = rest - gains[-1]
    gains = jnp.concatenate(gains + [jnp.zeros_like(rest)], axis=0).astype(BF)

    one, zero = with_one.at[64 + width :, :], with_first.at[64 + width :, :]
    states = (zero, one, two, three)
    for n, d in enumerate(loaded):
        for k in range(2):
            zero[:, lanes_of(d, k)] = (turned, swapped)[k][n][core]
    if near:
        border_load.wait()
        for n, (s, f) in enumerate(borders):
            states[s][:, span(f)] = bordering[n]

    for s, (low, high) in enumerate(spans):
        source = states[s]
        gain = column_of(gains, [s, 4 + s, 8 + s])
        for f in range(max(low - 1, 0), min(high + 1, frames)):
            values = source[:, span(f)].astype(F32)
            scale = lax.rsqrt(jnp.mean(values * values, axis=0, keepdims=True) + EPS)
            normed = (values * scale * gain).astype(BF)
            for step in (-1, 0, 1):
                if low <= f + step < high:
                    unfolded[rows_of(step), span(f + step)] = normed
        pltpu.make_async_copy(packs[0], weights.at[s], sem_w.at[s]).wait()
        if s < 3:
            load_weights(s + 1)
        if s == 0:
            skip_load.start()
        film = 1.0 + column_of(weights[s, width:, 0:width], [clip, 4 + clip])
        film = jnp.concatenate([film] * (high - low), axis=1)
        cols = span(low, high - low)
        taps = weights[s, 0:width, 0 : unfolded.shape[0]]
        mixed = jnp.dot(taps, unfolded[:, cols], preferred_element_type=F32) * film
        hidden = (mixed * (0.5 + 0.5 * jnp.tanh(0.5 * mixed))).astype(BF)
        projection = weights[s, 0:width, 3 * width - 64 :]
        if s < 2:
            with_one[64 : 64 + width, cols] = hidden
            right = with_one[0 : 64 + width, cols]
        else:
            if s == 2:
                skip_load.wait()
            beside = with_one if s == 2 else with_first
            beside[64 : 64 + width, cols] = hidden
            right = beside[:, cols]
            projection = jnp.concatenate([projection, skip[s - 2].T], axis=1)
        total = source[:, cols].astype(F32)
        total = (total + jnp.dot(projection, right, preferred_element_type=F32)).astype(BF)
        (one, two, three, last)[s][:, cols] = total
    for n, d in enumerate(dests):
        for k, out in enumerate((kept, given)):
            out[n] = last[:, lanes_of(d, k)]
    if borders and not near:
        for n, (s, f) in enumerate(borders):
            border_out[n] = states[s][:, span(f)]


def run_sections(
    spans, dests, borders, loaded, turned, swapped, weights, skip, gain, border=None
):
    levels = lax.axis_size("frame") // 2
    frames = 2 * levels
    width = gain.shape[1]
    columns = frames * LANES
    hbm = pl.BlockSpec(memory_space=pltpu.HBM)
    vmem = pl.BlockSpec(memory_space=pltpu.VMEM)
    given_out = [pltpu.VMEM((len(dests), width, LANES), BF)] * 2
    blocks = [*turned, *swapped]
    places = [pltpu.VMEM, pltpu.HBM, pltpu.HBM, pltpu.VMEM, pltpu.HBM]
    inputs = [pin([a], place)[0] for a, place in zip([*weights, skip], places, strict=True)]
    after = []
    if border is not None:
        after = pin([border], pltpu.HBM)
    elif borders:
        given_out.append(jax.ShapeDtypeStruct((len(borders), width, LANES), BF))
    flops = sum(high - low for low, high in spans) * LANES * 2 * 5 * width * width
    return pl.pallas_call(
        functools.partial(
            sections_kernel, spans, dests, borders, levels, width, loaded
        ),
        out_shape=given_out,
        in_specs=[vmem] * len(blocks)
        + [pl.BlockSpec(memory_space=place) for place in places]
        + [pl.BlockSpec(memory_space=pltpu.VMEM)]
        + [hbm] * len(after),
        out_specs=[vmem] * len(given_out),
        scratch_shapes=[
            pltpu.VMEM((4, width + FILM_ROWS, 4 * width), BF),
            pltpu.VMEM((2, width, width), BF),
            pltpu.VMEM((3 * width + 64, columns), BF),
            pltpu.VMEM((2 * width + 64, columns), BF),
            pltpu.VMEM((2 * width + 64, columns), BF),
            pltpu.VMEM((width, columns), BF),
            pltpu.VMEM((width, columns), BF),
            pltpu.VMEM((width, columns), BF),
            pltpu.VMEM((6, width, LANES), BF),
            pltpu.SemaphoreType.DMA((4,)),
            pltpu.SemaphoreType.DMA,
            pltpu.SemaphoreType.DMA,
        ],
        compiler_params=pltpu.CompilerParams(vmem_limit_bytes=40 << 20),
        cost_estimate=pl.CostEstimate(flops=flops, bytes_accessed=4 << 20, transcendentals=0),
        name="sections",
    )(*pin(blocks, pltpu.VMEM), *inputs, gain, *after)


IN_ORDER = (2, 3, 1, 0)
OUT_ORDER = (2, 3, 1, 0)
OUT_PARTS = ((0, (0, 1)), (1, (0, 1)), (3, (1,)), (2, (1,)), (3, (0,)), (2, (0,)))


def block_shards(clips, timesteps, gain, temporal_weight, film_weight, out_weight, skip_weight):
    levels = lax.axis_size("frame") // 2

    *cut, pack0 = pack_and_cut(
        timesteps, clips[0, 0], temporal_weight[0], out_weight[0], film_weight[0], levels
    )
    pack2 = swap_planes(pack0)
    turned = [turn(cut[d], d) for d in IN_ORDER]
    pack1 = swap_cores(pack0)
    pack2, *turned = lax.optimization_barrier((pack2, *turned))
    pack3 = swap_cores(pack2)
    swapped = [swap_cores(block) for block in turned]

    kept, given = run_sections(
        [(0, 2 * levels)] * 4,
        OUT_ORDER,
        None,
        IN_ORDER,
        turned,
        swapped,
        [pack0, pack1, pack2, pack3],
        skip_weight,
        gain,
    )
    swapped = swap_cores(given)
    back = []
    for d, halves in OUT_PARTS:
        n = OUT_ORDER.index(d)
        back.append(turn(jnp.stack([(kept, swapped)[k][n] for k in halves]), d))
    return join_blocks(back, OUT_PARTS)[None, None]


def solution(mesh):
    placed = (
        P("segment", "frame", None, None),
        P(),
        P(),
        P("segment", None, None, None),
        P("segment", None, None),
        P("segment", None, None),
        P(),
    )

    def run(*arrays):
        clips, gain = arrays[0], arrays[2]
        split = mesh.shape["frame"]
        fits = (
            clips.shape[1] == split == 8
            and clips.shape[3] == split * LANES
            and clips.shape[2] % 64 == 0
            and clips.shape[0] == gain.shape[0] == mesh.shape["segment"] == 4
        )
        return jax.shard_map(
            block_shards if fits else plain_shards,
            mesh=mesh,
            in_specs=placed,
            out_specs=P("segment", "frame", None, None),
            check_vma=False,
        )(*arrays)

    return run
```

```python
import functools
import math

import jax
import jax.numpy as jnp
from jax import lax
from jax.experimental import pallas as pl
from jax.experimental.pallas import tpu as pltpu
from jax.sharding import PartitionSpec as P

BF = jnp.bfloat16
F32 = jnp.float32
LANES = 128
EPS = 1e-05


def embed(timesteps, width):
    half = width // 2
    freq = jnp.exp(-math.log(10000.0) * jnp.arange(half, dtype=jnp.float32) / half)
    angle = timesteps.astype(jnp.float32)[:, None] * freq[None, :]
    return jnp.concatenate([jnp.sin(angle), jnp.cos(angle)], axis=-1).astype(jnp.bfloat16)


def exchange(array, axis, by):
    return lax.ppermute(array, axis, [(i, i ^ by) for i in range(lax.axis_size(axis))])


def plain_section(state, gain, taps, film, projection, extra):
    values = state.astype(F32)
    meansq = jnp.mean(values * values, axis=1, keepdims=True)
    normed = (values * lax.rsqrt(meansq + EPS) * gain[None, :, None]).astype(BF)
    padded = jnp.pad(normed, ((1, 1), (0, 0), (0, 0)))
    count = state.shape[0]
    mixed = sum(
        jnp.einsum("io,fip->fop", taps[tau], padded[tau : tau + count], preferred_element_type=F32)
        for tau in range(3)
    )
    hidden = jax.nn.silu(mixed * (1.0 + film[None, :, None])).astype(BF)
    total = values + jnp.einsum("io,fip->fop", projection, hidden, preferred_element_type=F32)
    if extra is not None:
        total = total + jnp.einsum("io,fip->fop", extra[0], extra[1], preferred_element_type=F32)
    return total.astype(BF)


def plain_shards(clips, timesteps, gain, temporal_weight, film_weight, out_weight, skip_weight):
    own = clips[0]
    pixels = own.shape[2]
    split = lax.axis_size("frame")
    pad = -pixels % split
    if pad:
        own = jnp.pad(own, ((0, 0), (0, 0), (0, pad)))
    state = lax.all_to_all(own, "frame", 2, 0, tiled=True)
    emb = embed(timesteps, clips.shape[2])
    film = jnp.dot(emb, film_weight[0], preferred_element_type=F32)
    taps = lax.all_gather(temporal_weight[0], "segment")
    projection = lax.all_gather(out_weight[0], "segment")
    films = lax.all_gather(film, "segment")
    micro = lax.axis_index("segment")
    first = state
    skips = {}
    for section in range(gain.shape[0]):
        extra = None
        if section == 2:
            extra = (skip_weight[0], skips[0])
        if section == 3:
            extra = (skip_weight[1], first)
        film_vec = lax.dynamic_index_in_dim(films[section], micro, 0, keepdims=False)
        state = plain_section(
            state, gain[section], taps[section], film_vec, projection[section], extra
        )
        skips[section] = state
    result = lax.all_to_all(state, "frame", 0, 2, tiled=True)
    return result[None, :, :, :pixels]


FILM_ROWS = 16
JOIN_STEPS = 4


def place():
    segment, frame = lax.axis_index("segment"), lax.axis_index("frame")
    return segment // 2, segment % 2, frame // 2, frame % 2


def devices():
    for segment in range(4):
        for frame in range(8):
            yield segment, frame, (segment // 2, segment % 2, frame // 2, frame % 2)


def move(array, rule):
    pairs = []
    for segment, frame, (y, c, z, x) in devices():
        y, c, z, x = rule(y, c, z, x)
        pairs.append((segment * 8 + frame, (2 * y + c) * 8 + 2 * z + x))
    return lax.ppermute(array, ("segment", "frame"), pairs)


def turn(array, by):
    return move(array, lambda y, c, z, x: (y, x, z ^ by, c))


def swap_cores(array):
    return move(array, lambda y, c, z, x: (y, 1 - c, z, x))


def swap_planes(array):
    return move(array, lambda y, c, z, x: (1 - y, c, z, x))


def pin(arrays, space):
    return [pltpu.with_memory_space_constraint(a, space) for a in arrays]


def pack_kernel(levels, times_ref, x_ref, taps_ref, projection_ref, film_ref, *outs):
    width = projection_ref.shape[0]
    pack = outs[levels]
    held = jnp.concatenate(
        [taps_ref[...].reshape(3 * width, width).T, projection_ref[...].T], axis=1
    )
    lane = lax.broadcasted_iota(jnp.int32, (8, width), 1)
    row = lax.broadcasted_iota(jnp.int32, (8, width), 0)
    half = width // 2
    index = jnp.where(lane < half, lane, lane - half).astype(F32)
    freq = jnp.exp(-math.log(10000.0) * index / half)
    times = jnp.zeros((8, width), jnp.int32)
    for m in range(4):
        times = jnp.where(row == m, times_ref[m], times)
    angle = times.astype(F32) * freq
    emb = jnp.where(lane < half, jnp.sin(angle), jnp.cos(angle)).astype(BF)
    film = jnp.dot(emb, film_ref[...], preferred_element_type=F32)
    high = film.astype(BF).astype(F32)
    rows = jnp.concatenate([high[0:4], (film - high)[0:4], jnp.zeros((8, width), F32)], axis=0)
    rows = jnp.concatenate([rows.astype(BF), jnp.zeros((FILM_ROWS, 3 * width), BF)], axis=1)
    pack[0:width] = held
    pack[width:] = rows
    z = lax.axis_index("frame") // 2
    for d in range(levels):
        for k in range(2):
            at = pl.multiple_of(((z ^ d) * 2 + k) * LANES, LANES)
            outs[d][k] = x_ref[:, pl.ds(at, LANES)]


def pack_and_cut(times, own, taps, projection, film_weight, levels):
    width = own.shape[0]
    vmem = pl.BlockSpec(memory_space=pltpu.VMEM)
    return pl.pallas_call(
        functools.partial(pack_kernel, levels),
        out_shape=[pltpu.VMEM((2, width, LANES), BF)] * levels
        + [pltpu.VMEM((width + FILM_ROWS, 4 * width), BF)],
        in_specs=[pl.BlockSpec(memory_space=pltpu.SMEM)] + [vmem] * 4,
        out_specs=[vmem] * (levels + 1),
        name="pack",
    )(times, own, taps, projection, film_weight)


def join_kernel(parts, *refs):
    blocks, out, joined, sem = refs[: len(parts)], *refs[len(parts) :]
    frame = lax.axis_index("frame")
    z, x = frame // 2, frame % 2
    stores = []
    step = joined.shape[0] // JOIN_STEPS
    for low in range(0, joined.shape[0], step):
        rows = pl.ds(low, step)
        for block, (d, halves) in zip(blocks, parts, strict=True):
            for n, k in enumerate(halves):
                at = pl.multiple_of(((z ^ d) * 2 + (x ^ k)) * LANES, LANES)
                joined[rows, pl.ds(at, LANES)] = block[n, rows]
        stores.append(pltpu.make_async_copy(joined.at[rows], out.at[rows], sem.at[low // step]))
        stores[-1].start()
    for store in stores:
        store.wait()


def join_blocks(blocks, parts):
    width = blocks[0].shape[1]
    columns = sum(len(halves) for _, halves in parts) * LANES
    vmem = pl.BlockSpec(memory_space=pltpu.VMEM)
    return pl.pallas_call(
        functools.partial(join_kernel, parts),
        out_shape=jax.ShapeDtypeStruct((width, columns), BF),
        in_specs=[vmem] * len(blocks),
        out_specs=pl.BlockSpec(memory_space=pltpu.HBM),
        scratch_shapes=[
            pltpu.VMEM((width, columns), BF),
            pltpu.SemaphoreType.DMA((JOIN_STEPS,)),
        ],
        name="join",
    )(*pin(blocks, pltpu.VMEM))


def sections_kernel(dests, levels, width, loaded, *refs):
    refs = list(refs)

    def take(count):
        taken = refs[:count]
        del refs[:count]
        return taken

    turned, swapped = take(len(loaded)), take(len(loaded))
    packs = take(4)
    skip_in, gain_ref = take(2)
    kept, given = take(2)
    weights, skip, around, with_one, with_first, two, three, last = take(8)
    sem_w, sem_s = take(2)
    y, core, z, x = place()
    clip = 2 * y + x
    segment = 2 * y + core
    frames = 2 * levels

    def load_weights(s):
        for b in range(4):

            @pl.when(segment ^ s == b)
            def _():
                pltpu.make_async_copy(packs[b], weights.at[s], sem_w.at[s]).start()

    load_weights(0)
    skip_load = pltpu.make_async_copy(skip_in, skip, sem_s)

    def lanes_of(d, k):
        slot = 2 * (z ^ d) + (core ^ k)
        return pl.ds(pl.multiple_of(slot * LANES, LANES), LANES)

    def span(f, count=1):
        return slice(f * LANES, (f + count) * LANES)

    zeros = jnp.zeros((width, LANES), BF)
    around[:, span(0)] = zeros
    around[:, span(frames + 1)] = zeros
    for ref in (with_one, with_first):
        ref[0:64, :] = jnp.zeros((64, frames * LANES), BF)

    def column_of(rows, chosen):
        at = lax.broadcasted_iota(jnp.int32, (16, LANES), 0)
        hit = functools.reduce(jnp.logical_or, [at == c for c in chosen])
        return lax.dot_general(
            rows,
            jnp.where(hit, 1.0, 0.0).astype(BF),
            (((0,), (0,)), ((), ())),
            preferred_element_type=F32,
        )

    gains = []
    rest = gain_ref[...]
    for _ in range(3):
        gains.append(rest.astype(BF).astype(F32))
        rest = rest - gains[-1]
    gains = jnp.concatenate(gains + [jnp.zeros_like(rest)], axis=0).astype(BF)

    one, zero = with_one.at[64 + width :, :], with_first.at[64 + width :, :]
    for n, d in enumerate(loaded):
        for k in range(2):
            zero[:, lanes_of(d, k)] = (turned, swapped)[k][n][core]

    for s in range(4):
        source, target = ((zero, one), (one, two), (two, three), (three, last))[s]
        gain = column_of(gains, [s, 4 + s, 8 + s])
        values = source[...].astype(F32)
        scale = lax.rsqrt(jnp.mean(values * values, axis=0, keepdims=True) + EPS)
        wide = jnp.concatenate([gain] * frames, axis=1)
        around[:, span(1, frames)] = (values * scale * wide).astype(BF)
        pltpu.make_async_copy(packs[0], weights.at[s], sem_w.at[s]).wait()
        if s < 3:
            load_weights(s + 1)
        if s == 0:
            skip_load.start()
        half = 0.5 + 0.5 * column_of(weights[s, width:, 0:width], [clip, 4 + clip])
        half = jnp.concatenate([half] * frames, axis=1)
        three_frames = jnp.concatenate(
            [around[:, span(tau, frames)] for tau in range(3)]
            + [jnp.zeros((64, frames * LANES), BF)],
            axis=0,
        )
        mixed = jnp.dot(
            weights[s, 0:width, 0 : 3 * width + 64], three_frames, preferred_element_type=F32
        )
        mixed = mixed * half
        beside = with_first if s == 3 else with_one
        beside[64 : 64 + width, :] = (mixed * (1.0 + jnp.tanh(mixed))).astype(BF)
        projection = weights[s, 0:width, 3 * width - 64 :]
        right = beside[0 : 64 + width, :]
        if s >= 2:
            if s == 2:
                skip_load.wait()
            projection = jnp.concatenate([projection, skip[s - 2].T], axis=1)
            right = beside[...]
        total = source[...].astype(F32)
        total = (total + jnp.dot(projection, right, preferred_element_type=F32)).astype(BF)
        target[...] = total
    for n, d in enumerate(dests):
        for k, out in enumerate((kept, given)):
            out[n] = last[:, lanes_of(d, k)]


def run_sections(dests, loaded, turned, swapped, weights, skip, gain):
    levels = lax.axis_size("frame") // 2
    frames = 2 * levels
    width = gain.shape[1]
    columns = frames * LANES
    vmem = pl.BlockSpec(memory_space=pltpu.VMEM)
    blocks = [*turned, *swapped]
    places = [pltpu.VMEM] * 4 + [pltpu.HBM]
    inputs = [pin([a], place)[0] for a, place in zip([*weights, skip], places, strict=True)]
    return pl.pallas_call(
        functools.partial(sections_kernel, dests, levels, width, loaded),
        out_shape=[pltpu.VMEM((len(dests), width, LANES), BF)] * 2,
        in_specs=[vmem] * len(blocks)
        + [pl.BlockSpec(memory_space=place) for place in places]
        + [vmem],
        out_specs=[vmem] * 2,
        scratch_shapes=[
            pltpu.VMEM((4, width + FILM_ROWS, 4 * width), BF),
            pltpu.VMEM((2, width, width), BF),
            pltpu.VMEM((width, columns + 2 * LANES), BF),
            pltpu.VMEM((2 * width + 64, columns), BF),
            pltpu.VMEM((2 * width + 64, columns), BF),
            pltpu.VMEM((width, columns), BF),
            pltpu.VMEM((width, columns), BF),
            pltpu.VMEM((width, columns), BF),
            pltpu.SemaphoreType.DMA((4,)),
            pltpu.SemaphoreType.DMA,
        ],
        compiler_params=pltpu.CompilerParams(vmem_limit_bytes=40 << 20),
        cost_estimate=pl.CostEstimate(
            flops=columns * 2 * 18 * width * width, bytes_accessed=4 << 20, transcendentals=0
        ),
        name="sections",
    )(*pin(blocks, pltpu.VMEM), *inputs, gain)


IN_ORDER = (2, 3, 1, 0)
OUT_ORDER = (2, 3, 1, 0)
OUT_PARTS = ((0, (0, 1)), (1, (0, 1)), (3, (1,)), (2, (1,)), (3, (0,)), (2, (0,)))


def block_shards(clips, timesteps, gain, temporal_weight, film_weight, out_weight, skip_weight):
    levels = lax.axis_size("frame") // 2

    *cut, pack0 = pack_and_cut(
        timesteps, clips[0, 0], temporal_weight[0], out_weight[0], film_weight[0], levels
    )
    pack2 = swap_planes(pack0)
    turned = [turn(cut[d], d) for d in IN_ORDER]
    pack1 = swap_cores(pack0)
    pack2, *turned = lax.optimization_barrier((pack2, *turned))
    pack3 = swap_cores(pack2)
    swapped = [swap_cores(block) for block in turned]

    weights = [pack0, pack1, pack2, pack3]
    kept, given = run_sections(
        OUT_ORDER, IN_ORDER, turned, swapped, weights, skip_weight, gain
    )
    swapped = swap_cores(given)
    back = []
    for d, halves in OUT_PARTS:
        n = OUT_ORDER.index(d)
        back.append(turn(jnp.stack([(kept, swapped)[k][n] for k in halves]), d))
    return join_blocks(back, OUT_PARTS)[None, None]


def solution(mesh):
    placed = (
        P("segment", "frame", None, None),
        P(),
        P(),
        P("segment", None, None, None),
        P("segment", None, None),
        P("segment", None, None),
        P(),
    )

    def run(*arrays):
        clips, gain = arrays[0], arrays[2]
        split = mesh.shape["frame"]
        fits = (
            clips.shape[1] == split == 8
            and clips.shape[3] == split * LANES
            and clips.shape[2] % 64 == 0
            and clips.shape[0] == gain.shape[0] == mesh.shape["segment"] == 4
        )
        return jax.shard_map(
            block_shards if fits else plain_shards,
            mesh=mesh,
            in_specs=placed,
            out_specs=P("segment", "frame", None, None),
            check_vma=False,
        )(*arrays)

    return run
```

```python
import functools
import math

import jax
import jax.numpy as jnp
from jax import lax
from jax.experimental import pallas as pl
from jax.experimental.pallas import tpu as pltpu
from jax.sharding import PartitionSpec as P

BF = jnp.bfloat16
F32 = jnp.float32
LANES = 128
EPS = 1e-05


def embed(timesteps, width):
    half = width // 2
    freq = jnp.exp(-math.log(10000.0) * jnp.arange(half, dtype=jnp.float32) / half)
    angle = timesteps.astype(jnp.float32)[:, None] * freq[None, :]
    return jnp.concatenate([jnp.sin(angle), jnp.cos(angle)], axis=-1).astype(jnp.bfloat16)


def exchange(array, axis, by):
    return lax.ppermute(array, axis, [(i, i ^ by) for i in range(lax.axis_size(axis))])


def plain_section(state, gain, taps, film, projection, extra):
    values = state.astype(F32)
    meansq = jnp.mean(values * values, axis=1, keepdims=True)
    normed = (values * lax.rsqrt(meansq + EPS) * gain[None, :, None]).astype(BF)
    padded = jnp.pad(normed, ((1, 1), (0, 0), (0, 0)))
    count = state.shape[0]
    mixed = sum(
        jnp.einsum("io,fip->fop", taps[tau], padded[tau : tau + count], preferred_element_type=F32)
        for tau in range(3)
    )
    hidden = jax.nn.silu(mixed * (1.0 + film[None, :, None])).astype(BF)
    total = values + jnp.einsum("io,fip->fop", projection, hidden, preferred_element_type=F32)
    if extra is not None:
        total = total + jnp.einsum("io,fip->fop", extra[0], extra[1], preferred_element_type=F32)
    return total.astype(BF)


def plain_shards(clips, timesteps, gain, temporal_weight, film_weight, out_weight, skip_weight):
    own = clips[0]
    pixels = own.shape[2]
    split = lax.axis_size("frame")
    pad = -pixels % split
    if pad:
        own = jnp.pad(own, ((0, 0), (0, 0), (0, pad)))
    state = lax.all_to_all(own, "frame", 2, 0, tiled=True)
    emb = embed(timesteps, clips.shape[2])
    film = jnp.dot(emb, film_weight[0], preferred_element_type=F32)
    taps = lax.all_gather(temporal_weight[0], "segment")
    projection = lax.all_gather(out_weight[0], "segment")
    films = lax.all_gather(film, "segment")
    micro = lax.axis_index("segment")
    first = state
    skips = {}
    for section in range(gain.shape[0]):
        extra = None
        if section == 2:
            extra = (skip_weight[0], skips[0])
        if section == 3:
            extra = (skip_weight[1], first)
        film_vec = lax.dynamic_index_in_dim(films[section], micro, 0, keepdims=False)
        state = plain_section(
            state, gain[section], taps[section], film_vec, projection[section], extra
        )
        skips[section] = state
    result = lax.all_to_all(state, "frame", 0, 2, tiled=True)
    return result[None, :, :, :pixels]


FILM_ROWS = 16
JOIN_STEPS = 4


def place():
    segment, frame = lax.axis_index("segment"), lax.axis_index("frame")
    return segment // 2, segment % 2, frame // 2, frame % 2


def devices():
    for segment in range(4):
        for frame in range(8):
            yield segment, frame, (segment // 2, segment % 2, frame // 2, frame % 2)


def move(array, rule):
    pairs = []
    for segment, frame, (y, c, z, x) in devices():
        y, c, z, x = rule(y, c, z, x)
        pairs.append((segment * 8 + frame, (2 * y + c) * 8 + 2 * z + x))
    return lax.ppermute(array, ("segment", "frame"), pairs)


def turn(array, by):
    return move(array, lambda y, c, z, x: (y, x, z ^ by, c))


def swap_cores(array):
    return move(array, lambda y, c, z, x: (y, 1 - c, z, x))


def swap_planes(array):
    return move(array, lambda y, c, z, x: (1 - y, c, z, x))


def pin(arrays, space):
    return [pltpu.with_memory_space_constraint(a, space) for a in arrays]


def pack_kernel(levels, times_ref, x_ref, taps_ref, projection_ref, film_ref, *outs):
    width = projection_ref.shape[0]
    pack = outs[levels]
    held = jnp.concatenate(
        [taps_ref[...].reshape(3 * width, width).T, projection_ref[...].T], axis=1
    )
    lane = lax.broadcasted_iota(jnp.int32, (8, width), 1)
    row = lax.broadcasted_iota(jnp.int32, (8, width), 0)
    half = width // 2
    index = jnp.where(lane < half, lane, lane - half).astype(F32)
    freq = jnp.exp(-math.log(10000.0) * index / half)
    times = jnp.zeros((8, width), jnp.int32)
    for m in range(4):
        times = jnp.where(row == m, times_ref[m], times)
    angle = times.astype(F32) * freq
    emb = jnp.where(lane < half, jnp.sin(angle), jnp.cos(angle)).astype(BF)
    film = jnp.dot(emb, film_ref[...], preferred_element_type=F32)
    high = film.astype(BF).astype(F32)
    rows = jnp.concatenate([high[0:4], (film - high)[0:4], jnp.zeros((8, width), F32)], axis=0)
    rows = jnp.concatenate([rows.astype(BF), jnp.zeros((FILM_ROWS, 3 * width), BF)], axis=1)
    pack[0:width] = held
    pack[width:] = rows
    z = lax.axis_index("frame") // 2
    for d in range(levels):
        for k in range(2):
            at = pl.multiple_of(((z ^ d) * 2 + k) * LANES, LANES)
            outs[d][k] = x_ref[:, pl.ds(at, LANES)]


def pack_and_cut(times, own, taps, projection, film_weight, levels):
    width = own.shape[0]
    vmem = pl.BlockSpec(memory_space=pltpu.VMEM)
    return pl.pallas_call(
        functools.partial(pack_kernel, levels),
        out_shape=[pltpu.VMEM((2, width, LANES), BF)] * levels
        + [pltpu.VMEM((width + FILM_ROWS, 4 * width), BF)],
        in_specs=[pl.BlockSpec(memory_space=pltpu.SMEM)] + [vmem] * 4,
        out_specs=[vmem] * (levels + 1),
        name="pack",
    )(times, own, taps, projection, film_weight)


def pick_kernel(*refs):
    other = 1 - lax.axis_index("segment") % 2
    for n, block in enumerate(refs[:-1]):
        refs[-1][n] = block[other]


def pick_others(blocks):
    vmem = pl.BlockSpec(memory_space=pltpu.VMEM)
    return pl.pallas_call(
        pick_kernel,
        out_shape=pltpu.VMEM((len(blocks), *blocks[0].shape[1:]), BF),
        in_specs=[vmem] * len(blocks),
        out_specs=vmem,
        name="pick",
    )(*pin(blocks, pltpu.VMEM))


def join_kernel(parts, *refs):
    blocks, out, joined, sem = refs[: len(parts)], *refs[len(parts) :]
    frame = lax.axis_index("frame")
    z, x = frame // 2, frame % 2
    stores = []
    step = joined.shape[0] // JOIN_STEPS
    for low in range(0, joined.shape[0], step):
        rows = pl.ds(low, step)
        for block, (d, halves) in zip(blocks, parts, strict=True):
            for n, k in enumerate(halves):
                at = pl.multiple_of(((z ^ d) * 2 + (x ^ k)) * LANES, LANES)
                joined[rows, pl.ds(at, LANES)] = block[n, rows]
        stores.append(pltpu.make_async_copy(joined.at[rows], out.at[rows], sem.at[low // step]))
        stores[-1].start()
    for store in stores:
        store.wait()


def join_blocks(blocks, parts):
    width = blocks[0].shape[1]
    columns = sum(len(halves) for _, halves in parts) * LANES
    vmem = pl.BlockSpec(memory_space=pltpu.VMEM)
    return pl.pallas_call(
        functools.partial(join_kernel, parts),
        out_shape=jax.ShapeDtypeStruct((width, columns), BF),
        in_specs=[vmem] * len(blocks),
        out_specs=pl.BlockSpec(memory_space=pltpu.HBM),
        scratch_shapes=[
            pltpu.VMEM((width, columns), BF),
            pltpu.SemaphoreType.DMA((JOIN_STEPS,)),
        ],
        name="join",
    )(*pin(blocks, pltpu.VMEM))


def sections_kernel(dests, levels, width, loaded, *refs):
    refs = list(refs)

    def take(count):
        taken = refs[:count]
        del refs[:count]
        return taken

    turned, (swapped,) = take(len(loaded)), take(1)
    packs = take(4)
    skip_in, gain_ref = take(2)
    kept, given = take(2)
    weights, skip, around, with_one, with_first, two, three, last = take(8)
    sem_w, sem_s = take(2)
    y, core, z, x = place()
    clip = 2 * y + x
    segment = 2 * y + core
    frames = 2 * levels

    def load_weights(s):
        for b in range(4):

            @pl.when(segment ^ s == b)
            def _():
                pltpu.make_async_copy(packs[b], weights.at[s], sem_w.at[s]).start()

    load_weights(0)
    skip_load = pltpu.make_async_copy(skip_in, skip, sem_s)

    def lanes_of(d, k):
        slot = 2 * (z ^ d) + (core ^ k)
        return pl.ds(pl.multiple_of(slot * LANES, LANES), LANES)

    def span(f, count=1):
        return slice(f * LANES, (f + count) * LANES)

    zeros = jnp.zeros((width, LANES), BF)
    around[:, span(0)] = zeros
    around[:, span(frames + 1)] = zeros
    for ref in (with_one, with_first):
        ref[0:64, :] = jnp.zeros((64, frames * LANES), BF)

    def column_of(rows, chosen):
        at = lax.broadcasted_iota(jnp.int32, (16, LANES), 0)
        hit = functools.reduce(jnp.logical_or, [at == c for c in chosen])
        return lax.dot_general(
            rows,
            jnp.where(hit, 1.0, 0.0).astype(BF),
            (((0,), (0,)), ((), ())),
            preferred_element_type=F32,
        )

    gains = []
    rest = gain_ref[...]
    for _ in range(3):
        gains.append(rest.astype(BF).astype(F32))
        rest = rest - gains[-1]
    gains = jnp.concatenate(gains + [jnp.zeros_like(rest)], axis=0).astype(BF)

    one, zero = with_one.at[64 + width :, :], with_first.at[64 + width :, :]
    for n, d in enumerate(loaded):
        for k in range(2):
            zero[:, lanes_of(d, k)] = turned[n][core] if k == 0 else swapped[n]

    for s in range(4):
        source, target = ((zero, one), (one, two), (two, three), (three, last))[s]
        gain = column_of(gains, [s, 4 + s, 8 + s])
        values = source[...].astype(F32)
        scale = lax.rsqrt(jnp.mean(values * values, axis=0, keepdims=True) + EPS)
        wide = jnp.concatenate([gain] * frames, axis=1)
        around[:, span(1, frames)] = (values * scale * wide).astype(BF)
        pltpu.make_async_copy(packs[0], weights.at[s], sem_w.at[s]).wait()
        if s < 3:
            load_weights(s + 1)
        if s == 0:
            skip_load.start()
        half = 0.5 + 0.5 * column_of(weights[s, width:, 0:width], [clip, 4 + clip])
        half = jnp.concatenate([half] * frames, axis=1)
        three_frames = jnp.concatenate(
            [around[:, span(tau, frames)] for tau in range(3)]
            + [jnp.zeros((64, frames * LANES), BF)],
            axis=0,
        )
        mixed = jnp.dot(
            weights[s, 0:width, 0 : 3 * width + 64], three_frames, preferred_element_type=F32
        )
        mixed = mixed * half
        beside = with_first if s == 3 else with_one
        beside[64 : 64 + width, :] = (mixed * (1.0 + jnp.tanh(mixed))).astype(BF)
        projection = weights[s, 0:width, 3 * width - 64 :]
        right = beside[0 : 64 + width, :]
        if s >= 2:
            if s == 2:
                skip_load.wait()
            projection = jnp.concatenate([projection, skip[s - 2].T], axis=1)
            right = beside[...]
        total = source[...].astype(F32)
        total = (total + jnp.dot(projection, right, preferred_element_type=F32)).astype(BF)
        target[...] = total
    for n, d in enumerate(dests):
        for k, out in enumerate((kept, given)):
            out[n] = last[:, lanes_of(d, k)]


def run_sections(dests, loaded, turned, swapped, weights, skip, gain):
    levels = lax.axis_size("frame") // 2
    frames = 2 * levels
    width = gain.shape[1]
    columns = frames * LANES
    vmem = pl.BlockSpec(memory_space=pltpu.VMEM)
    blocks = [*turned, swapped]
    places = [pltpu.VMEM, pltpu.HBM, pltpu.VMEM, pltpu.VMEM, pltpu.HBM]
    inputs = [pin([a], place)[0] for a, place in zip([*weights, skip], places, strict=True)]
    return pl.pallas_call(
        functools.partial(sections_kernel, dests, levels, width, loaded),
        out_shape=[pltpu.VMEM((len(dests), width, LANES), BF)] * 2,
        in_specs=[vmem] * len(blocks)
        + [pl.BlockSpec(memory_space=place) for place in places]
        + [vmem],
        out_specs=[vmem] * 2,
        scratch_shapes=[
            pltpu.VMEM((4, width + FILM_ROWS, 4 * width), BF),
            pltpu.VMEM((2, width, width), BF),
            pltpu.VMEM((width, columns + 2 * LANES), BF),
            pltpu.VMEM((2 * width + 64, columns), BF),
            pltpu.VMEM((2 * width + 64, columns), BF),
            pltpu.VMEM((width, columns), BF),
            pltpu.VMEM((width, columns), BF),
            pltpu.VMEM((width, columns), BF),
            pltpu.SemaphoreType.DMA((4,)),
            pltpu.SemaphoreType.DMA,
        ],
        compiler_params=pltpu.CompilerParams(vmem_limit_bytes=40 << 20),
        cost_estimate=pl.CostEstimate(
            flops=columns * 2 * 18 * width * width, bytes_accessed=4 << 20, transcendentals=0
        ),
        name="sections",
    )(*pin(blocks, pltpu.VMEM), *inputs, gain)


IN_ORDER = (2, 3, 1, 0)
OUT_ORDER = (2, 3, 1, 0)
OUT_PARTS = ((0, (0, 1)), (1, (0, 1)), (3, (1,)), (2, (1,)), (3, (0,)), (2, (0,)))


def block_shards(clips, timesteps, gain, temporal_weight, film_weight, out_weight, skip_weight):
    levels = lax.axis_size("frame") // 2

    *cut, pack0 = pack_and_cut(
        timesteps, clips[0, 0], temporal_weight[0], out_weight[0], film_weight[0], levels
    )
    pack2 = swap_planes(pack0)
    turned = [turn(cut[d], d) for d in IN_ORDER]
    pack1 = swap_cores(pack0)
    picked = pick_others(turned)
    pack2, picked = lax.optimization_barrier((pack2, picked))
    swapped = swap_cores(picked)
    pack3 = swap_cores(pack2)

    weights = [pack0, pack1, pack2, pack3]
    kept, given = run_sections(
        OUT_ORDER, IN_ORDER, turned, swapped, weights, skip_weight, gain
    )
    swapped = swap_cores(given)
    back = []
    for d, halves in OUT_PARTS:
        n = OUT_ORDER.index(d)
        back.append(turn(jnp.stack([(kept, swapped)[k][n] for k in halves]), d))
    return join_blocks(back, OUT_PARTS)[None, None]


def solution(mesh):
    placed = (
        P("segment", "frame", None, None),
        P(),
        P(),
        P("segment", None, None, None),
        P("segment", None, None),
        P("segment", None, None),
        P(),
    )

    def run(*arrays):
        clips, gain = arrays[0], arrays[2]
        split = mesh.shape["frame"]
        fits = (
            clips.shape[1] == split == 8
            and clips.shape[3] == split * LANES
            and clips.shape[2] % 64 == 0
            and clips.shape[0] == gain.shape[0] == mesh.shape["segment"] == 4
        )
        return jax.shard_map(
            block_shards if fits else plain_shards,
            mesh=mesh,
            in_specs=placed,
            out_specs=P("segment", "frame", None, None),
            check_vma=False,
        )(*arrays)

    return run
```

```python
import functools
import math

import jax
import jax.numpy as jnp
from jax import lax
from jax.experimental import pallas as pl
from jax.experimental.pallas import tpu as pltpu
from jax.sharding import PartitionSpec as P

BF = jnp.bfloat16
F32 = jnp.float32
LANES = 128
EPS = 1e-05


def embed(timesteps, width):
    half = width // 2
    freq = jnp.exp(-math.log(10000.0) * jnp.arange(half, dtype=jnp.float32) / half)
    angle = timesteps.astype(jnp.float32)[:, None] * freq[None, :]
    return jnp.concatenate([jnp.sin(angle), jnp.cos(angle)], axis=-1).astype(jnp.bfloat16)


def exchange(array, axis, by):
    return lax.ppermute(array, axis, [(i, i ^ by) for i in range(lax.axis_size(axis))])


def plain_section(state, gain, taps, film, projection, extra):
    values = state.astype(F32)
    meansq = jnp.mean(values * values, axis=1, keepdims=True)
    normed = (values * lax.rsqrt(meansq + EPS) * gain[None, :, None]).astype(BF)
    padded = jnp.pad(normed, ((1, 1), (0, 0), (0, 0)))
    count = state.shape[0]
    mixed = sum(
        jnp.einsum("io,fip->fop", taps[tau], padded[tau : tau + count], preferred_element_type=F32)
        for tau in range(3)
    )
    hidden = jax.nn.silu(mixed * (1.0 + film[None, :, None])).astype(BF)
    total = values + jnp.einsum("io,fip->fop", projection, hidden, preferred_element_type=F32)
    if extra is not None:
        total = total + jnp.einsum("io,fip->fop", extra[0], extra[1], preferred_element_type=F32)
    return total.astype(BF)


def plain_shards(clips, timesteps, gain, temporal_weight, film_weight, out_weight, skip_weight):
    own = clips[0]
    pixels = own.shape[2]
    split = lax.axis_size("frame")
    pad = -pixels % split
    if pad:
        own = jnp.pad(own, ((0, 0), (0, 0), (0, pad)))
    state = lax.all_to_all(own, "frame", 2, 0, tiled=True)
    emb = embed(timesteps, clips.shape[2])
    film = jnp.dot(emb, film_weight[0], preferred_element_type=F32)
    taps = lax.all_gather(temporal_weight[0], "segment")
    projection = lax.all_gather(out_weight[0], "segment")
    films = lax.all_gather(film, "segment")
    micro = lax.axis_index("segment")
    first = state
    skips = {}
    for section in range(gain.shape[0]):
        extra = None
        if section == 2:
            extra = (skip_weight[0], skips[0])
        if section == 3:
            extra = (skip_weight[1], first)
        film_vec = lax.dynamic_index_in_dim(films[section], micro, 0, keepdims=False)
        state = plain_section(
            state, gain[section], taps[section], film_vec, projection[section], extra
        )
        skips[section] = state
    result = lax.all_to_all(state, "frame", 0, 2, tiled=True)
    return result[None, :, :, :pixels]


FILM_ROWS = 16
JOIN_STEPS = 4


def place():
    segment, frame = lax.axis_index("segment"), lax.axis_index("frame")
    return segment // 2, segment % 2, frame // 2, frame % 2


def devices():
    for segment in range(4):
        for frame in range(8):
            yield segment, frame, (segment // 2, segment % 2, frame // 2, frame % 2)


def move(array, rule):
    pairs = []
    for segment, frame, (y, c, z, x) in devices():
        y, c, z, x = rule(y, c, z, x)
        pairs.append((segment * 8 + frame, (2 * y + c) * 8 + 2 * z + x))
    return lax.ppermute(array, ("segment", "frame"), pairs)


def turn(array, by):
    return move(array, lambda y, c, z, x: (y, x, z ^ by, c))


def swap_cores(array):
    return move(array, lambda y, c, z, x: (y, 1 - c, z, x))


def swap_planes(array):
    return move(array, lambda y, c, z, x: (1 - y, c, z, x))


def pin(arrays, space):
    return [pltpu.with_memory_space_constraint(a, space) for a in arrays]


def pack_kernel(levels, times_ref, x_ref, taps_ref, projection_ref, film_ref, *outs):
    width = projection_ref.shape[0]
    pack = outs[levels]
    held = jnp.concatenate(
        [taps_ref[...].reshape(3 * width, width).T, projection_ref[...].T], axis=1
    )
    lane = lax.broadcasted_iota(jnp.int32, (8, width), 1)
    row = lax.broadcasted_iota(jnp.int32, (8, width), 0)
    half = width // 2
    index = jnp.where(lane < half, lane, lane - half).astype(F32)
    freq = jnp.exp(-math.log(10000.0) * index / half)
    times = jnp.zeros((8, width), jnp.int32)
    for m in range(4):
        times = jnp.where(row == m, times_ref[m], times)
    angle = times.astype(F32) * freq
    emb = jnp.where(lane < half, jnp.sin(angle), jnp.cos(angle)).astype(BF)
    film = jnp.dot(emb, film_ref[...], preferred_element_type=F32)
    high = film.astype(BF).astype(F32)
    rows = jnp.concatenate([high[0:4], (film - high)[0:4], jnp.zeros((8, width), F32)], axis=0)
    rows = jnp.concatenate([rows.astype(BF), jnp.zeros((FILM_ROWS, 3 * width), BF)], axis=1)
    pack[0:width] = held
    pack[width:] = rows
    z = lax.axis_index("frame") // 2
    for d in range(levels):
        for k in range(2):
            at = pl.multiple_of(((z ^ d) * 2 + k) * LANES, LANES)
            outs[d][k] = x_ref[:, pl.ds(at, LANES)]


def pack_and_cut(times, own, taps, projection, film_weight, levels):
    width = own.shape[0]
    vmem = pl.BlockSpec(memory_space=pltpu.VMEM)
    return pl.pallas_call(
        functools.partial(pack_kernel, levels),
        out_shape=[pltpu.VMEM((2, width, LANES), BF)] * levels
        + [pltpu.VMEM((width + FILM_ROWS, 4 * width), BF)],
        in_specs=[pl.BlockSpec(memory_space=pltpu.SMEM)] + [vmem] * 4,
        out_specs=[vmem] * (levels + 1),
        name="pack",
    )(times, own, taps, projection, film_weight)


def pick_kernel(*refs):
    other = 1 - lax.axis_index("segment") % 2
    for n, block in enumerate(refs[:-1]):
        refs[-1][n] = block[other]


def pick_others(blocks):
    vmem = pl.BlockSpec(memory_space=pltpu.VMEM)
    return pl.pallas_call(
        pick_kernel,
        out_shape=pltpu.VMEM((len(blocks), *blocks[0].shape[1:]), BF),
        in_specs=[vmem] * len(blocks),
        out_specs=vmem,
        name="pick",
    )(*pin(blocks, pltpu.VMEM))


def join_kernel(parts, *refs):
    blocks, out, joined, sem = refs[: len(parts)], *refs[len(parts) :]
    frame = lax.axis_index("frame")
    z, x = frame // 2, frame % 2
    stores = []
    step = joined.shape[0] // JOIN_STEPS
    for low in range(0, joined.shape[0], step):
        rows = pl.ds(low, step)
        for block, (d, halves) in zip(blocks, parts, strict=True):
            for n, k in enumerate(halves):
                at = pl.multiple_of(((z ^ d) * 2 + (x ^ k)) * LANES, LANES)
                joined[rows, pl.ds(at, LANES)] = block[n, rows]
        stores.append(pltpu.make_async_copy(joined.at[rows], out.at[rows], sem.at[low // step]))
        stores[-1].start()
    for store in stores:
        store.wait()


def join_blocks(blocks, parts):
    width = blocks[0].shape[1]
    columns = sum(len(halves) for _, halves in parts) * LANES
    vmem = pl.BlockSpec(memory_space=pltpu.VMEM)
    return pl.pallas_call(
        functools.partial(join_kernel, parts),
        out_shape=jax.ShapeDtypeStruct((width, columns), BF),
        in_specs=[vmem] * len(blocks),
        out_specs=pl.BlockSpec(memory_space=pltpu.HBM),
        scratch_shapes=[
            pltpu.VMEM((width, columns), BF),
            pltpu.SemaphoreType.DMA((JOIN_STEPS,)),
        ],
        name="join",
    )(*pin(blocks, pltpu.VMEM))


def sections_kernel(dests, levels, width, loaded, *refs):
    refs = list(refs)

    def take(count):
        taken = refs[:count]
        del refs[:count]
        return taken

    turned, (swapped,) = take(len(loaded)), take(1)
    packs = take(4)
    skip_in, gain_ref = take(2)
    kept, given = take(2)
    weights, skip, around, with_one, with_first, two, three, last = take(8)
    sem_w, sem_s = take(2)
    y, core, z, x = place()
    clip = 2 * y + x
    segment = 2 * y + core
    frames = 2 * levels

    def load_weights(s):
        for b in range(4):

            @pl.when(segment ^ s == b)
            def _():
                pltpu.make_async_copy(packs[b], weights.at[s], sem_w.at[s]).start()

    def wait_weights(s):
        pltpu.make_async_copy(packs[0], weights.at[s], sem_w.at[s]).wait()

    for s in range(4):
        load_weights(s)
    skip_load = pltpu.make_async_copy(skip_in, skip, sem_s)
    skip_load.start()

    def lanes_of(d, k):
        slot = 2 * (z ^ d) + (core ^ k)
        return pl.ds(pl.multiple_of(slot * LANES, LANES), LANES)

    def span(f, count=1):
        return slice(f * LANES, (f + count) * LANES)

    zeros = jnp.zeros((width, LANES), BF)
    around[:, span(0)] = zeros
    around[:, span(frames + 1)] = zeros
    for ref in (with_one, with_first):
        ref[0:64, :] = jnp.zeros((64, frames * LANES), BF)

    def column_of(rows, chosen):
        at = lax.broadcasted_iota(jnp.int32, (16, LANES), 0)
        hit = functools.reduce(jnp.logical_or, [at == c for c in chosen])
        return lax.dot_general(
            rows,
            jnp.where(hit, 1.0, 0.0).astype(BF),
            (((0,), (0,)), ((), ())),
            preferred_element_type=F32,
        )

    gains = []
    rest = gain_ref[...]
    for _ in range(3):
        gains.append(rest.astype(BF).astype(F32))
        rest = rest - gains[-1]
    gains = jnp.concatenate(gains + [jnp.zeros_like(rest)], axis=0).astype(BF)

    one, zero = with_one.at[64 + width :, :], with_first.at[64 + width :, :]
    for n, d in enumerate(loaded):
        for k in range(2):
            zero[:, lanes_of(d, k)] = turned[n][core] if k == 0 else swapped[n]

    gain_columns = [column_of(gains, [s, 4 + s, 8 + s]) for s in range(4)]
    for s in range(4):
        source, target = ((zero, one), (one, two), (two, three), (three, last))[s]
        gain = gain_columns[s]
        values = source[...].astype(F32)
        scale = lax.rsqrt(jnp.mean(values * values, axis=0, keepdims=True) + EPS)
        wide = jnp.concatenate([gain] * frames, axis=1)
        around[:, span(1, frames)] = (values * scale * wide).astype(BF)
        if s == 0:
            wait_weights(0)
        if s == 1:
            for later in range(1, 4):
                wait_weights(later)
            skip_load.wait()
        half = 0.5 + 0.5 * column_of(weights[s, width:, 0:width], [clip, 4 + clip])
        half = jnp.concatenate([half] * frames, axis=1)
        three_frames = jnp.concatenate(
            [around[:, span(tau, frames)] for tau in range(3)]
            + [jnp.zeros((64, frames * LANES), BF)],
            axis=0,
        )
        mixed = jnp.dot(
            weights[s, 0:width, 0 : 3 * width + 64], three_frames, preferred_element_type=F32
        )
        mixed = mixed * half
        beside = with_first if s == 3 else with_one
        beside[64 : 64 + width, :] = (mixed * (1.0 + jnp.tanh(mixed))).astype(BF)
        projection = weights[s, 0:width, 3 * width - 64 :]
        right = beside[0 : 64 + width, :]
        if s >= 2:
            projection = jnp.concatenate([projection, skip[s - 2].T], axis=1)
            right = beside[...]
        total = source[...].astype(F32)
        total = (total + jnp.dot(projection, right, preferred_element_type=F32)).astype(BF)
        target[...] = total
    for n, d in enumerate(dests):
        for k, out in enumerate((kept, given)):
            out[n] = last[:, lanes_of(d, k)]


def run_sections(dests, loaded, turned, swapped, weights, skip, gain):
    levels = lax.axis_size("frame") // 2
    frames = 2 * levels
    width = gain.shape[1]
    columns = frames * LANES
    vmem = pl.BlockSpec(memory_space=pltpu.VMEM)
    blocks = [*turned, swapped]
    places = [pltpu.VMEM, pltpu.HBM, pltpu.VMEM, pltpu.VMEM, pltpu.HBM]
    inputs = [pin([a], place)[0] for a, place in zip([*weights, skip], places, strict=True)]
    return pl.pallas_call(
        functools.partial(sections_kernel, dests, levels, width, loaded),
        out_shape=[pltpu.VMEM((len(dests), width, LANES), BF)] * 2,
        in_specs=[vmem] * len(blocks)
        + [pl.BlockSpec(memory_space=place) for place in places]
        + [vmem],
        out_specs=[vmem] * 2,
        scratch_shapes=[
            pltpu.VMEM((4, width + FILM_ROWS, 4 * width), BF),
            pltpu.VMEM((2, width, width), BF),
            pltpu.VMEM((width, columns + 2 * LANES), BF),
            pltpu.VMEM((2 * width + 64, columns), BF),
            pltpu.VMEM((2 * width + 64, columns), BF),
            pltpu.VMEM((width, columns), BF),
            pltpu.VMEM((width, columns), BF),
            pltpu.VMEM((width, columns), BF),
            pltpu.SemaphoreType.DMA((4,)),
            pltpu.SemaphoreType.DMA,
        ],
        compiler_params=pltpu.CompilerParams(vmem_limit_bytes=40 << 20),
        cost_estimate=pl.CostEstimate(
            flops=columns * 2 * 18 * width * width, bytes_accessed=4 << 20, transcendentals=0
        ),
        name="sections",
    )(*pin(blocks, pltpu.VMEM), *inputs, gain)


IN_ORDER = (2, 3, 1, 0)
OUT_ORDER = (2, 3, 1, 0)
OUT_PARTS = ((0, (0, 1)), (1, (0, 1)), (3, (1,)), (2, (1,)), (3, (0,)), (2, (0,)))


def block_shards(clips, timesteps, gain, temporal_weight, film_weight, out_weight, skip_weight):
    levels = lax.axis_size("frame") // 2

    *cut, pack0 = pack_and_cut(
        timesteps, clips[0, 0], temporal_weight[0], out_weight[0], film_weight[0], levels
    )
    pack2 = swap_planes(pack0)
    turned = [turn(cut[d], d) for d in IN_ORDER]
    pack1 = swap_cores(pack0)
    picked = pick_others(turned)
    pack2, picked = lax.optimization_barrier((pack2, picked))
    swapped = swap_cores(picked)
    pack3 = swap_cores(pack2)

    weights = [pack0, pack1, pack2, pack3]
    kept, given = run_sections(
        OUT_ORDER, IN_ORDER, turned, swapped, weights, skip_weight, gain
    )
    swapped = swap_cores(given)
    back = []
    for d, halves in OUT_PARTS:
        n = OUT_ORDER.index(d)
        back.append(turn(jnp.stack([(kept, swapped)[k][n] for k in halves]), d))
    return join_blocks(back, OUT_PARTS)[None, None]


def solution(mesh):
    placed = (
        P("segment", "frame", None, None),
        P(),
        P(),
        P("segment", None, None, None),
        P("segment", None, None),
        P("segment", None, None),
        P(),
    )

    def run(*arrays):
        clips, gain = arrays[0], arrays[2]
        split = mesh.shape["frame"]
        fits = (
            clips.shape[1] == split == 8
            and clips.shape[3] == split * LANES
            and clips.shape[2] % 64 == 0
            and clips.shape[0] == gain.shape[0] == mesh.shape["segment"] == 4
        )
        return jax.shard_map(
            block_shards if fits else plain_shards,
            mesh=mesh,
            in_specs=placed,
            out_specs=P("segment", "frame", None, None),
            check_vma=False,
        )(*arrays)

    return run
```

```python
import functools
import math

import jax
import jax.numpy as jnp
from jax import lax
from jax.experimental import pallas as pl
from jax.experimental.pallas import tpu as pltpu
from jax.sharding import PartitionSpec as P

BF = jnp.bfloat16
F32 = jnp.float32
LANES = 128
EPS = 1e-05


def embed(timesteps, width):
    half = width // 2
    freq = jnp.exp(-math.log(10000.0) * jnp.arange(half, dtype=jnp.float32) / half)
    angle = timesteps.astype(jnp.float32)[:, None] * freq[None, :]
    return jnp.concatenate([jnp.sin(angle), jnp.cos(angle)], axis=-1).astype(jnp.bfloat16)


def exchange(array, axis, by):
    return lax.ppermute(array, axis, [(i, i ^ by) for i in range(lax.axis_size(axis))])


def plain_section(state, gain, taps, film, projection, extra):
    values = state.astype(F32)
    meansq = jnp.mean(values * values, axis=1, keepdims=True)
    normed = (values * lax.rsqrt(meansq + EPS) * gain[None, :, None]).astype(BF)
    padded = jnp.pad(normed, ((1, 1), (0, 0), (0, 0)))
    count = state.shape[0]
    mixed = sum(
        jnp.einsum("io,fip->fop", taps[tau], padded[tau : tau + count], preferred_element_type=F32)
        for tau in range(3)
    )
    hidden = jax.nn.silu(mixed * (1.0 + film[None, :, None])).astype(BF)
    total = values + jnp.einsum("io,fip->fop", projection, hidden, preferred_element_type=F32)
    if extra is not None:
        total = total + jnp.einsum("io,fip->fop", extra[0], extra[1], preferred_element_type=F32)
    return total.astype(BF)


def plain_shards(clips, timesteps, gain, temporal_weight, film_weight, out_weight, skip_weight):
    own = clips[0]
    pixels = own.shape[2]
    split = lax.axis_size("frame")
    pad = -pixels % split
    if pad:
        own = jnp.pad(own, ((0, 0), (0, 0), (0, pad)))
    state = lax.all_to_all(own, "frame", 2, 0, tiled=True)
    emb = embed(timesteps, clips.shape[2])
    film = jnp.dot(emb, film_weight[0], preferred_element_type=F32)
    taps = lax.all_gather(temporal_weight[0], "segment")
    projection = lax.all_gather(out_weight[0], "segment")
    films = lax.all_gather(film, "segment")
    micro = lax.axis_index("segment")
    first = state
    skips = {}
    for section in range(gain.shape[0]):
        extra = None
        if section == 2:
            extra = (skip_weight[0], skips[0])
        if section == 3:
            extra = (skip_weight[1], first)
        film_vec = lax.dynamic_index_in_dim(films[section], micro, 0, keepdims=False)
        state = plain_section(
            state, gain[section], taps[section], film_vec, projection[section], extra
        )
        skips[section] = state
    result = lax.all_to_all(state, "frame", 0, 2, tiled=True)
    return result[None, :, :, :pixels]


FILM_ROWS = 16
JOIN_STEPS = 4


def place():
    segment, frame = lax.axis_index("segment"), lax.axis_index("frame")
    return segment // 2, segment % 2, frame // 2, frame % 2


def devices():
    for segment in range(4):
        for frame in range(8):
            yield segment, frame, (segment // 2, segment % 2, frame // 2, frame % 2)


def move(array, rule):
    pairs = []
    for segment, frame, (y, c, z, x) in devices():
        y, c, z, x = rule(y, c, z, x)
        pairs.append((segment * 8 + frame, (2 * y + c) * 8 + 2 * z + x))
    return lax.ppermute(array, ("segment", "frame"), pairs)


def turn(array, by):
    return move(array, lambda y, c, z, x: (y, x, z ^ by, c))


def swap_cores(array):
    return move(array, lambda y, c, z, x: (y, 1 - c, z, x))


def swap_planes(array):
    return move(array, lambda y, c, z, x: (1 - y, c, z, x))


def pin(arrays, space):
    return [pltpu.with_memory_space_constraint(a, space) for a in arrays]


def pack_kernel(levels, times_ref, x_ref, taps_ref, projection_ref, film_ref, *outs):
    width = projection_ref.shape[0]
    pack = outs[levels]
    held = jnp.concatenate(
        [taps_ref[...].reshape(3 * width, width).T, projection_ref[...].T], axis=1
    )
    lane = lax.broadcasted_iota(jnp.int32, (8, width), 1)
    row = lax.broadcasted_iota(jnp.int32, (8, width), 0)
    half = width // 2
    index = jnp.where(lane < half, lane, lane - half).astype(F32)
    freq = jnp.exp(-math.log(10000.0) * index / half)
    times = jnp.zeros((8, width), jnp.int32)
    for m in range(4):
        times = jnp.where(row == m, times_ref[m], times)
    angle = times.astype(F32) * freq
    emb = jnp.where(lane < half, jnp.sin(angle), jnp.cos(angle)).astype(BF)
    film = jnp.dot(emb, film_ref[...], preferred_element_type=F32)
    high = film.astype(BF).astype(F32)
    rows = jnp.concatenate([high[0:4], (film - high)[0:4], jnp.zeros((8, width), F32)], axis=0)
    rows = jnp.concatenate([rows.astype(BF), jnp.zeros((FILM_ROWS, 3 * width), BF)], axis=1)
    pack[0:width] = held
    pack[width:] = rows
    z = lax.axis_index("frame") // 2
    for d in range(levels):
        for k in range(2):
            at = pl.multiple_of(((z ^ d) * 2 + k) * LANES, LANES)
            outs[d][k] = x_ref[:, pl.ds(at, LANES)]


def pack_and_cut(times, own, taps, projection, film_weight, levels):
    width = own.shape[0]
    vmem = pl.BlockSpec(memory_space=pltpu.VMEM)
    return pl.pallas_call(
        functools.partial(pack_kernel, levels),
        out_shape=[pltpu.VMEM((2, width, LANES), BF)] * levels
        + [pltpu.VMEM((width + FILM_ROWS, 4 * width), BF)],
        in_specs=[pl.BlockSpec(memory_space=pltpu.SMEM)] + [vmem] * 4,
        out_specs=[vmem] * (levels + 1),
        name="pack",
    )(times, own, taps, projection, film_weight)


def pick_kernel(*refs):
    other = 1 - lax.axis_index("segment") % 2
    for n, block in enumerate(refs[:-1]):
        refs[-1][n] = block[other]


def pick_others(blocks):
    vmem = pl.BlockSpec(memory_space=pltpu.VMEM)
    return pl.pallas_call(
        pick_kernel,
        out_shape=pltpu.VMEM((len(blocks), *blocks[0].shape[1:]), BF),
        in_specs=[vmem] * len(blocks),
        out_specs=vmem,
        name="pick",
    )(*pin(blocks, pltpu.VMEM))


def join_kernel(parts, *refs):
    blocks, out, joined, sem = refs[: len(parts)], *refs[len(parts) :]
    frame = lax.axis_index("frame")
    z, x = frame // 2, frame % 2
    stores = []
    step = joined.shape[0] // JOIN_STEPS
    for low in range(0, joined.shape[0], step):
        rows = pl.ds(low, step)
        for block, (d, halves) in zip(blocks, parts, strict=True):
            for n, k in enumerate(halves):
                at = pl.multiple_of(((z ^ d) * 2 + (x ^ k)) * LANES, LANES)
                joined[rows, pl.ds(at, LANES)] = block[n, rows]
        stores.append(pltpu.make_async_copy(joined.at[rows], out.at[rows], sem.at[low // step]))
        stores[-1].start()
    for store in stores:
        store.wait()


def join_blocks(blocks, parts):
    width = blocks[0].shape[1]
    columns = sum(len(halves) for _, halves in parts) * LANES
    vmem = pl.BlockSpec(memory_space=pltpu.VMEM)
    return pl.pallas_call(
        functools.partial(join_kernel, parts),
        out_shape=jax.ShapeDtypeStruct((width, columns), BF),
        in_specs=[vmem] * len(blocks),
        out_specs=pl.BlockSpec(memory_space=pltpu.HBM),
        scratch_shapes=[
            pltpu.VMEM((width, columns), BF),
            pltpu.SemaphoreType.DMA((JOIN_STEPS,)),
        ],
        name="join",
    )(*pin(blocks, pltpu.VMEM))


def sections_kernel(dests, levels, width, loaded, *refs):
    refs = list(refs)

    def take(count):
        taken = refs[:count]
        del refs[:count]
        return taken

    turned, (swapped,) = take(len(loaded)), take(1)
    packs = take(4)
    skip_in, gain_ref = take(2)
    kept, given = take(2)
    weights, skip, around, with_one, with_first, two, three = take(7)
    sem_w, sem_s = take(2)
    y, core, z, x = place()
    clip = 2 * y + x
    segment = 2 * y + core
    frames = 2 * levels

    def load_weights(s):
        for b in range(4):

            @pl.when(segment ^ s == b)
            def _():
                pltpu.make_async_copy(packs[b], weights.at[s], sem_w.at[s]).start()

    def wait_weights(s):
        pltpu.make_async_copy(packs[0], weights.at[s], sem_w.at[s]).wait()

    for s in range(4):
        load_weights(s)
    skip_load = pltpu.make_async_copy(skip_in, skip, sem_s)
    skip_load.start()

    def lanes_of(d, k):
        slot = 2 * (z ^ d) + (core ^ k)
        return pl.ds(pl.multiple_of(slot * LANES, LANES), LANES)

    def span(f, count=1):
        return slice(f * LANES, (f + count) * LANES)

    zeros = jnp.zeros((width, LANES), BF)
    around[:, span(0)] = zeros
    around[:, span(frames + 1)] = zeros
    for ref in (with_one, with_first):
        ref[0:64, :] = jnp.zeros((64, frames * LANES), BF)

    def column_of(rows, chosen):
        at = lax.broadcasted_iota(jnp.int32, (16, LANES), 0)
        hit = functools.reduce(jnp.logical_or, [at == c for c in chosen])
        return lax.dot_general(
            rows,
            jnp.where(hit, 1.0, 0.0).astype(BF),
            (((0,), (0,)), ((), ())),
            preferred_element_type=F32,
        )

    gains = []
    rest = gain_ref[...]
    for _ in range(3):
        gains.append(rest.astype(BF).astype(F32))
        rest = rest - gains[-1]
    gains = jnp.concatenate(gains + [jnp.zeros_like(rest)], axis=0).astype(BF)

    one, zero = with_one.at[64 + width :, :], with_first.at[64 + width :, :]
    for n, d in enumerate(loaded):
        for k in range(2):
            zero[:, lanes_of(d, k)] = turned[n][core] if k == 0 else swapped[n]

    gain_columns = [column_of(gains, [s, 4 + s, 8 + s]) for s in range(4)]
    for s in range(4):
        source, target = ((zero, one), (one, two), (two, three), (three, None))[s]
        gain = gain_columns[s]
        values = source[...].astype(F32)
        scale = lax.rsqrt(jnp.mean(values * values, axis=0, keepdims=True) + EPS)
        wide = jnp.concatenate([gain] * frames, axis=1)
        around[:, span(1, frames)] = (values * scale * wide).astype(BF)
        if s == 0:
            wait_weights(0)
        if s == 1:
            for later in range(1, 4):
                wait_weights(later)
            skip_load.wait()
        half = 0.5 + 0.5 * column_of(weights[s, width:, 0:width], [clip, 4 + clip])
        half = jnp.concatenate([half] * frames, axis=1)
        three_frames = jnp.concatenate(
            [around[:, span(tau, frames)] for tau in range(3)]
            + [jnp.zeros((64, frames * LANES), BF)],
            axis=0,
        )
        mixed = jnp.dot(
            weights[s, 0:width, 0 : 3 * width + 64], three_frames, preferred_element_type=F32
        )
        mixed = mixed * half
        beside = with_first if s == 3 else with_one
        beside[64 : 64 + width, :] = (mixed * (1.0 + jnp.tanh(mixed))).astype(BF)
        projection = weights[s, 0:width, 3 * width - 64 :]
        right = beside[0 : 64 + width, :]
        if s >= 2:
            projection = jnp.concatenate([projection, skip[s - 2].T], axis=1)
            right = beside[...]
        total = source[...].astype(F32)
        total = (total + jnp.dot(projection, right, preferred_element_type=F32)).astype(BF)
        if s < 3:
            target[...] = total
        else:
            outcome = total
    for c in range(2):

        @pl.when(core == c)
        def _():
            for f in range(frames):
                level = z ^ (f // 2)
                at = sum(jnp.where(level == d, n, 0) for n, d in enumerate(dests))
                (kept, given)[(f + c) % 2][at] = outcome[:, span(f)]


def run_sections(dests, loaded, turned, swapped, weights, skip, gain):
    levels = lax.axis_size("frame") // 2
    frames = 2 * levels
    width = gain.shape[1]
    columns = frames * LANES
    vmem = pl.BlockSpec(memory_space=pltpu.VMEM)
    blocks = [*turned, swapped]
    places = [pltpu.VMEM, pltpu.HBM, pltpu.VMEM, pltpu.VMEM, pltpu.HBM]
    inputs = [pin([a], place)[0] for a, place in zip([*weights, skip], places, strict=True)]
    return pl.pallas_call(
        functools.partial(sections_kernel, dests, levels, width, loaded),
        out_shape=[pltpu.VMEM((len(dests), width, LANES), BF)] * 2,
        in_specs=[vmem] * len(blocks)
        + [pl.BlockSpec(memory_space=place) for place in places]
        + [vmem],
        out_specs=[vmem] * 2,
        scratch_shapes=[
            pltpu.VMEM((4, width + FILM_ROWS, 4 * width), BF),
            pltpu.VMEM((2, width, width), BF),
            pltpu.VMEM((width, columns + 2 * LANES), BF),
            pltpu.VMEM((2 * width + 64, columns), BF),
            pltpu.VMEM((2 * width + 64, columns), BF),
            pltpu.VMEM((width, columns), BF),
            pltpu.VMEM((width, columns), BF),
            pltpu.SemaphoreType.DMA((4,)),
            pltpu.SemaphoreType.DMA,
        ],
        compiler_params=pltpu.CompilerParams(vmem_limit_bytes=40 << 20),
        cost_estimate=pl.CostEstimate(
            flops=columns * 2 * 18 * width * width, bytes_accessed=4 << 20, transcendentals=0
        ),
        name="sections",
    )(*pin(blocks, pltpu.VMEM), *inputs, gain)


IN_ORDER = (2, 3, 1, 0)
OUT_ORDER = (2, 3, 1, 0)
OUT_PARTS = ((0, (0, 1)), (1, (0, 1)), (3, (1,)), (2, (1,)), (3, (0,)), (2, (0,)))


def block_shards(clips, timesteps, gain, temporal_weight, film_weight, out_weight, skip_weight):
    levels = lax.axis_size("frame") // 2

    *cut, pack0 = pack_and_cut(
        timesteps, clips[0, 0], temporal_weight[0], out_weight[0], film_weight[0], levels
    )
    pack2 = swap_planes(pack0)
    turned = [turn(cut[d], d) for d in IN_ORDER]
    pack1 = swap_cores(pack0)
    picked = pick_others(turned)
    pack2, picked = lax.optimization_barrier((pack2, picked))
    swapped = swap_cores(picked)
    pack3 = swap_cores(pack2)

    weights = [pack0, pack1, pack2, pack3]
    kept, given = run_sections(
        OUT_ORDER, IN_ORDER, turned, swapped, weights, skip_weight, gain
    )
    swapped = swap_cores(given)
    back = []
    for d, halves in OUT_PARTS:
        n = OUT_ORDER.index(d)
        back.append(turn(jnp.stack([(kept, swapped)[k][n] for k in halves]), d))
    return join_blocks(back, OUT_PARTS)[None, None]


def solution(mesh):
    placed = (
        P("segment", "frame", None, None),
        P(),
        P(),
        P("segment", None, None, None),
        P("segment", None, None),
        P("segment", None, None),
        P(),
    )

    def run(*arrays):
        clips, gain = arrays[0], arrays[2]
        split = mesh.shape["frame"]
        fits = (
            clips.shape[1] == split == 8
            and clips.shape[3] == split * LANES
            and clips.shape[2] % 64 == 0
            and clips.shape[0] == gain.shape[0] == mesh.shape["segment"] == 4
        )
        return jax.shard_map(
            block_shards if fits else plain_shards,
            mesh=mesh,
            in_specs=placed,
            out_specs=P("segment", "frame", None, None),
            check_vma=False,
        )(*arrays)

    return run
```

```python
import functools
import math

import jax
import jax.numpy as jnp
from jax import lax
from jax.experimental import pallas as pl
from jax.experimental.pallas import tpu as pltpu
from jax.sharding import PartitionSpec as P

BF = jnp.bfloat16
F32 = jnp.float32
LANES = 128
EPS = 1e-05


def embed(timesteps, width):
    half = width // 2
    freq = jnp.exp(-math.log(10000.0) * jnp.arange(half, dtype=jnp.float32) / half)
    angle = timesteps.astype(jnp.float32)[:, None] * freq[None, :]
    return jnp.concatenate([jnp.sin(angle), jnp.cos(angle)], axis=-1).astype(jnp.bfloat16)


def exchange(array, axis, by):
    return lax.ppermute(array, axis, [(i, i ^ by) for i in range(lax.axis_size(axis))])


def plain_section(state, gain, taps, film, projection, extra):
    values = state.astype(F32)
    meansq = jnp.mean(values * values, axis=1, keepdims=True)
    normed = (values * lax.rsqrt(meansq + EPS) * gain[None, :, None]).astype(BF)
    padded = jnp.pad(normed, ((1, 1), (0, 0), (0, 0)))
    count = state.shape[0]
    mixed = sum(
        jnp.einsum("io,fip->fop", taps[tau], padded[tau : tau + count], preferred_element_type=F32)
        for tau in range(3)
    )
    hidden = jax.nn.silu(mixed * (1.0 + film[None, :, None])).astype(BF)
    total = values + jnp.einsum("io,fip->fop", projection, hidden, preferred_element_type=F32)
    if extra is not None:
        total = total + jnp.einsum("io,fip->fop", extra[0], extra[1], preferred_element_type=F32)
    return total.astype(BF)


def plain_shards(clips, timesteps, gain, temporal_weight, film_weight, out_weight, skip_weight):
    own = clips[0]
    pixels = own.shape[2]
    split = lax.axis_size("frame")
    pad = -pixels % split
    if pad:
        own = jnp.pad(own, ((0, 0), (0, 0), (0, pad)))
    state = lax.all_to_all(own, "frame", 2, 0, tiled=True)
    emb = embed(timesteps, clips.shape[2])
    film = jnp.dot(emb, film_weight[0], preferred_element_type=F32)
    taps = lax.all_gather(temporal_weight[0], "segment")
    projection = lax.all_gather(out_weight[0], "segment")
    films = lax.all_gather(film, "segment")
    micro = lax.axis_index("segment")
    first = state
    skips = {}
    for section in range(gain.shape[0]):
        extra = None
        if section == 2:
            extra = (skip_weight[0], skips[0])
        if section == 3:
            extra = (skip_weight[1], first)
        film_vec = lax.dynamic_index_in_dim(films[section], micro, 0, keepdims=False)
        state = plain_section(
            state, gain[section], taps[section], film_vec, projection[section], extra
        )
        skips[section] = state
    result = lax.all_to_all(state, "frame", 0, 2, tiled=True)
    return result[None, :, :, :pixels]


FILM_ROWS = 16
JOIN_STEPS = 4


def place():
    segment, frame = lax.axis_index("segment"), lax.axis_index("frame")
    return segment // 2, segment % 2, frame // 2, frame % 2


def devices():
    for segment in range(4):
        for frame in range(8):
            yield segment, frame, (segment // 2, segment % 2, frame // 2, frame % 2)


def move(array, rule):
    pairs = []
    for segment, frame, (y, c, z, x) in devices():
        y, c, z, x = rule(y, c, z, x)
        pairs.append((segment * 8 + frame, (2 * y + c) * 8 + 2 * z + x))
    return lax.ppermute(array, ("segment", "frame"), pairs)


def turn(array, by):
    return move(array, lambda y, c, z, x: (y, x, z ^ by, c))


def swap_cores(array):
    return move(array, lambda y, c, z, x: (y, 1 - c, z, x))


def swap_planes(array):
    return move(array, lambda y, c, z, x: (1 - y, c, z, x))


def pin(arrays, space):
    return [pltpu.with_memory_space_constraint(a, space) for a in arrays]


def pack_kernel(levels, times_ref, x_ref, taps_ref, projection_ref, film_ref, *outs):
    width = projection_ref.shape[0]
    pack = outs[levels]
    held = jnp.concatenate(
        [taps_ref[...].reshape(3 * width, width).T, projection_ref[...].T], axis=1
    )
    lane = lax.broadcasted_iota(jnp.int32, (8, width), 1)
    row = lax.broadcasted_iota(jnp.int32, (8, width), 0)
    half = width // 2
    index = jnp.where(lane < half, lane, lane - half).astype(F32)
    freq = jnp.exp(-math.log(10000.0) * index / half)
    times = jnp.zeros((8, width), jnp.int32)
    for m in range(4):
        times = jnp.where(row == m, times_ref[m], times)
    angle = times.astype(F32) * freq
    emb = jnp.where(lane < half, jnp.sin(angle), jnp.cos(angle)).astype(BF)
    film = jnp.dot(emb, film_ref[...], preferred_element_type=F32)
    high = film.astype(BF).astype(F32)
    rows = jnp.concatenate([high[0:4], (film - high)[0:4], jnp.zeros((8, width), F32)], axis=0)
    rows = jnp.concatenate([rows.astype(BF), jnp.zeros((FILM_ROWS, 3 * width), BF)], axis=1)
    pack[0:width] = held
    pack[width:] = rows
    z = lax.axis_index("frame") // 2
    for d in range(levels):
        for k in range(2):
            at = pl.multiple_of(((z ^ d) * 2 + k) * LANES, LANES)
            outs[d][k] = x_ref[:, pl.ds(at, LANES)]


def pack_and_cut(times, own, taps, projection, film_weight, levels):
    width = own.shape[0]
    vmem = pl.BlockSpec(memory_space=pltpu.VMEM)
    return pl.pallas_call(
        functools.partial(pack_kernel, levels),
        out_shape=[pltpu.VMEM((2, width, LANES), BF)] * levels
        + [pltpu.VMEM((width + FILM_ROWS, 4 * width), BF)],
        in_specs=[pl.BlockSpec(memory_space=pltpu.SMEM)] + [vmem] * 4,
        out_specs=[vmem] * (levels + 1),
        name="pack",
    )(times, own, taps, projection, film_weight)


def pick_kernel(*refs):
    other = 1 - lax.axis_index("segment") % 2
    for n, block in enumerate(refs[:-1]):
        refs[-1][n] = block[other]


def pick_others(blocks):
    vmem = pl.BlockSpec(memory_space=pltpu.VMEM)
    return pl.pallas_call(
        pick_kernel,
        out_shape=pltpu.VMEM((len(blocks), *blocks[0].shape[1:]), BF),
        in_specs=[vmem] * len(blocks),
        out_specs=vmem,
        name="pick",
    )(*pin(blocks, pltpu.VMEM))


def join_kernel(parts, *refs):
    blocks, out, joined, sem = refs[: len(parts)], *refs[len(parts) :]
    frame = lax.axis_index("frame")
    z, x = frame // 2, frame % 2
    stores = []
    step = joined.shape[0] // JOIN_STEPS
    for low in range(0, joined.shape[0], step):
        rows = pl.ds(low, step)
        for block, (d, halves) in zip(blocks, parts, strict=True):
            for n, k in enumerate(halves):
                at = pl.multiple_of(((z ^ d) * 2 + (x ^ k)) * LANES, LANES)
                joined[rows, pl.ds(at, LANES)] = block[n, rows]
        stores.append(pltpu.make_async_copy(joined.at[rows], out.at[rows], sem.at[low // step]))
        stores[-1].start()
    for store in stores:
        store.wait()


def join_blocks(blocks, parts):
    width = blocks[0].shape[1]
    columns = sum(len(halves) for _, halves in parts) * LANES
    vmem = pl.BlockSpec(memory_space=pltpu.VMEM)
    return pl.pallas_call(
        functools.partial(join_kernel, parts),
        out_shape=jax.ShapeDtypeStruct((width, columns), BF),
        in_specs=[vmem] * len(blocks),
        out_specs=pl.BlockSpec(memory_space=pltpu.HBM),
        scratch_shapes=[
            pltpu.VMEM((width, columns), BF),
            pltpu.SemaphoreType.DMA((JOIN_STEPS,)),
        ],
        name="join",
    )(*pin(blocks, pltpu.VMEM))


def sections_kernel(dests, levels, width, loaded, *refs):
    refs = list(refs)

    def take(count):
        taken = refs[:count]
        del refs[:count]
        return taken

    turned, (swapped,) = take(len(loaded)), take(1)
    packs = take(4)
    skip_in, gain_ref = take(2)
    kept, given = take(2)
    weights, skip, around, with_one, with_first, two, three = take(7)
    sem_w, sem_s = take(2)
    y, core, z, x = place()
    clip = 2 * y + x
    segment = 2 * y + core
    frames = 2 * levels

    def load_weights(s):
        for b in range(4):

            @pl.when(segment ^ s == b)
            def _():
                pltpu.make_async_copy(packs[b], weights.at[s], sem_w.at[s]).start()

    def wait_weights(s):
        pltpu.make_async_copy(packs[0], weights.at[s], sem_w.at[s]).wait()

    for s in range(4):
        load_weights(s)
    skip_load = pltpu.make_async_copy(skip_in, skip, sem_s)
    skip_load.start()

    def lanes_of(d, k):
        slot = 2 * (z ^ d) + (core ^ k)
        return pl.ds(pl.multiple_of(slot * LANES, LANES), LANES)

    def span(f, count=1):
        return slice(f * LANES, (f + count) * LANES)

    zeros = jnp.zeros((width, LANES), BF)
    around[:, span(0)] = zeros
    around[:, span(frames + 1)] = zeros
    for ref in (with_one, with_first):
        ref[0:64, :] = jnp.zeros((64, frames * LANES), BF)

    def column_of(rows, chosen):
        at = lax.broadcasted_iota(jnp.int32, (16, LANES), 0)
        hit = functools.reduce(jnp.logical_or, [at == c for c in chosen])
        return lax.dot_general(
            rows,
            jnp.where(hit, 1.0, 0.0).astype(BF),
            (((0,), (0,)), ((), ())),
            preferred_element_type=F32,
        )

    gains = []
    rest = gain_ref[...]
    for _ in range(3):
        gains.append(rest.astype(BF).astype(F32))
        rest = rest - gains[-1]
    gains = jnp.concatenate(gains + [jnp.zeros_like(rest)], axis=0).astype(BF)

    one, zero = with_one.at[64 + width :, :], with_first.at[64 + width :, :]
    for n, d in enumerate(loaded):
        for k in range(2):
            zero[:, lanes_of(d, k)] = turned[n][core] if k == 0 else swapped[n]

    gain_columns = [column_of(gains, [s, 4 + s, 8 + s]) for s in range(4)]
    for s in range(4):
        source, target = ((zero, one), (one, two), (two, three), (three, None))[s]
        gain = gain_columns[s]
        values = source[...].astype(F32)
        scale = lax.rsqrt(jnp.mean(values * values, axis=0, keepdims=True) + EPS)
        wide = jnp.concatenate([gain] * frames, axis=1)
        around[:, span(1, frames)] = (values * scale * wide).astype(BF)
        if s == 0:
            wait_weights(0)
        if s == 1:
            for later in range(1, 4):
                wait_weights(later)
            skip_load.wait()
            turned_skip = [skip[n].T for n in range(2)]
        half = 0.5 + 0.5 * column_of(weights[s, width:, 0:width], [clip, 4 + clip])
        half = jnp.concatenate([half] * frames, axis=1)
        three_frames = jnp.concatenate(
            [around[:, span(tau, frames)] for tau in range(3)]
            + [jnp.zeros((64, frames * LANES), BF)],
            axis=0,
        )
        mixed = jnp.dot(
            weights[s, 0:width, 0 : 3 * width + 64], three_frames, preferred_element_type=F32
        )
        mixed = mixed * half
        beside = with_first if s == 3 else with_one
        beside[64 : 64 + width, :] = (mixed * (1.0 + jnp.tanh(mixed))).astype(BF)
        projection = weights[s, 0:width, 3 * width - 64 :]
        right = beside[0 : 64 + width, :]
        if s >= 2:
            projection = jnp.concatenate([projection, turned_skip[s - 2]], axis=1)
            right = beside[...]
        total = source[...].astype(F32)
        total = (total + jnp.dot(projection, right, preferred_element_type=F32)).astype(BF)
        if s < 3:
            target[...] = total
        else:
            outcome = total
    for c in range(2):

        @pl.when(core == c)
        def _():
            for f in range(frames):
                level = z ^ (f // 2)
                at = sum(jnp.where(level == d, n, 0) for n, d in enumerate(dests))
                (kept, given)[(f + c) % 2][at] = outcome[:, span(f)]


def run_sections(dests, loaded, turned, swapped, weights, skip, gain):
    levels = lax.axis_size("frame") // 2
    frames = 2 * levels
    width = gain.shape[1]
    columns = frames * LANES
    vmem = pl.BlockSpec(memory_space=pltpu.VMEM)
    blocks = [*turned, swapped]
    places = [pltpu.VMEM, pltpu.HBM, pltpu.VMEM, pltpu.VMEM, pltpu.HBM]
    inputs = [pin([a], place)[0] for a, place in zip([*weights, skip], places, strict=True)]
    return pl.pallas_call(
        functools.partial(sections_kernel, dests, levels, width, loaded),
        out_shape=[pltpu.VMEM((len(dests), width, LANES), BF)] * 2,
        in_specs=[vmem] * len(blocks)
        + [pl.BlockSpec(memory_space=place) for place in places]
        + [vmem],
        out_specs=[vmem] * 2,
        scratch_shapes=[
            pltpu.VMEM((4, width + FILM_ROWS, 4 * width), BF),
            pltpu.VMEM((2, width, width), BF),
            pltpu.VMEM((width, columns + 2 * LANES), BF),
            pltpu.VMEM((2 * width + 64, columns), BF),
            pltpu.VMEM((2 * width + 64, columns), BF),
            pltpu.VMEM((width, columns), BF),
            pltpu.VMEM((width, columns), BF),
            pltpu.SemaphoreType.DMA((4,)),
            pltpu.SemaphoreType.DMA,
        ],
        compiler_params=pltpu.CompilerParams(vmem_limit_bytes=40 << 20),
        cost_estimate=pl.CostEstimate(
            flops=columns * 2 * 18 * width * width, bytes_accessed=4 << 20, transcendentals=0
        ),
        name="sections",
    )(*pin(blocks, pltpu.VMEM), *inputs, gain)


IN_ORDER = (2, 3, 1, 0)
OUT_ORDER = (2, 3, 1, 0)
OUT_PARTS = ((0, (0, 1)), (1, (0, 1)), (3, (1,)), (2, (1,)), (3, (0,)), (2, (0,)))


def block_shards(clips, timesteps, gain, temporal_weight, film_weight, out_weight, skip_weight):
    levels = lax.axis_size("frame") // 2

    *cut, pack0 = pack_and_cut(
        timesteps, clips[0, 0], temporal_weight[0], out_weight[0], film_weight[0], levels
    )
    pack2 = swap_planes(pack0)
    turned = [turn(cut[d], d) for d in IN_ORDER]
    pack1 = swap_cores(pack0)
    picked = pick_others(turned)
    pack2, picked = lax.optimization_barrier((pack2, picked))
    swapped = swap_cores(picked)
    pack3 = swap_cores(pack2)

    weights = [pack0, pack1, pack2, pack3]
    kept, given = run_sections(
        OUT_ORDER, IN_ORDER, turned, swapped, weights, skip_weight, gain
    )
    swapped = swap_cores(given)
    back = []
    for d, halves in OUT_PARTS:
        n = OUT_ORDER.index(d)
        back.append(turn(jnp.stack([(kept, swapped)[k][n] for k in halves]), d))
    return join_blocks(back, OUT_PARTS)[None, None]


def solution(mesh):
    placed = (
        P("segment", "frame", None, None),
        P(),
        P(),
        P("segment", None, None, None),
        P("segment", None, None),
        P("segment", None, None),
        P(),
    )

    def run(*arrays):
        clips, gain = arrays[0], arrays[2]
        split = mesh.shape["frame"]
        fits = (
            clips.shape[1] == split == 8
            and clips.shape[3] == split * LANES
            and clips.shape[2] % 64 == 0
            and clips.shape[0] == gain.shape[0] == mesh.shape["segment"] == 4
        )
        return jax.shard_map(
            block_shards if fits else plain_shards,
            mesh=mesh,
            in_specs=placed,
            out_specs=P("segment", "frame", None, None),
            check_vma=False,
        )(*arrays)

    return run
```

```python
import functools
import math

import jax
import jax.numpy as jnp
from jax import lax
from jax.experimental import pallas as pl
from jax.experimental.pallas import tpu as pltpu
from jax.sharding import PartitionSpec as P

BF = jnp.bfloat16
F32 = jnp.float32
LANES = 128
EPS = 1e-05


def embed(timesteps, width):
    half = width // 2
    freq = jnp.exp(-math.log(10000.0) * jnp.arange(half, dtype=jnp.float32) / half)
    angle = timesteps.astype(jnp.float32)[:, None] * freq[None, :]
    return jnp.concatenate([jnp.sin(angle), jnp.cos(angle)], axis=-1).astype(jnp.bfloat16)


def exchange(array, axis, by):
    return lax.ppermute(array, axis, [(i, i ^ by) for i in range(lax.axis_size(axis))])


def plain_section(state, gain, taps, film, projection, extra):
    values = state.astype(F32)
    meansq = jnp.mean(values * values, axis=1, keepdims=True)
    normed = (values * lax.rsqrt(meansq + EPS) * gain[None, :, None]).astype(BF)
    padded = jnp.pad(normed, ((1, 1), (0, 0), (0, 0)))
    count = state.shape[0]
    mixed = sum(
        jnp.einsum("io,fip->fop", taps[tau], padded[tau : tau + count], preferred_element_type=F32)
        for tau in range(3)
    )
    hidden = jax.nn.silu(mixed * (1.0 + film[None, :, None])).astype(BF)
    total = values + jnp.einsum("io,fip->fop", projection, hidden, preferred_element_type=F32)
    if extra is not None:
        total = total + jnp.einsum("io,fip->fop", extra[0], extra[1], preferred_element_type=F32)
    return total.astype(BF)


def plain_shards(clips, timesteps, gain, temporal_weight, film_weight, out_weight, skip_weight):
    own = clips[0]
    pixels = own.shape[2]
    split = lax.axis_size("frame")
    pad = -pixels % split
    if pad:
        own = jnp.pad(own, ((0, 0), (0, 0), (0, pad)))
    state = lax.all_to_all(own, "frame", 2, 0, tiled=True)
    emb = embed(timesteps, clips.shape[2])
    film = jnp.dot(emb, film_weight[0], preferred_element_type=F32)
    taps = lax.all_gather(temporal_weight[0], "segment")
    projection = lax.all_gather(out_weight[0], "segment")
    films = lax.all_gather(film, "segment")
    micro = lax.axis_index("segment")
    first = state
    skips = {}
    for section in range(gain.shape[0]):
        extra = None
        if section == 2:
            extra = (skip_weight[0], skips[0])
        if section == 3:
            extra = (skip_weight[1], first)
        film_vec = lax.dynamic_index_in_dim(films[section], micro, 0, keepdims=False)
        state = plain_section(
            state, gain[section], taps[section], film_vec, projection[section], extra
        )
        skips[section] = state
    result = lax.all_to_all(state, "frame", 0, 2, tiled=True)
    return result[None, :, :, :pixels]


FILM_ROWS = 16
JOIN_STEPS = 2


def place():
    segment, frame = lax.axis_index("segment"), lax.axis_index("frame")
    return segment // 2, segment % 2, frame // 2, frame % 2


def devices():
    for segment in range(4):
        for frame in range(8):
            yield segment, frame, (segment // 2, segment % 2, frame // 2, frame % 2)


def move(array, rule):
    pairs = []
    for segment, frame, (y, c, z, x) in devices():
        y, c, z, x = rule(y, c, z, x)
        pairs.append((segment * 8 + frame, (2 * y + c) * 8 + 2 * z + x))
    return lax.ppermute(array, ("segment", "frame"), pairs)


def turn(array, by):
    return move(array, lambda y, c, z, x: (y, x, z ^ by, c))


def swap_cores(array):
    return move(array, lambda y, c, z, x: (y, 1 - c, z, x))


def swap_planes(array):
    return move(array, lambda y, c, z, x: (1 - y, c, z, x))


def pin(arrays, space):
    return [pltpu.with_memory_space_constraint(a, space) for a in arrays]


def pack_kernel(levels, times_ref, x_ref, taps_ref, projection_ref, film_ref, *outs):
    width = projection_ref.shape[0]
    pack = outs[levels]
    held = jnp.concatenate(
        [taps_ref[...].reshape(3 * width, width).T, projection_ref[...].T], axis=1
    )
    lane = lax.broadcasted_iota(jnp.int32, (8, width), 1)
    row = lax.broadcasted_iota(jnp.int32, (8, width), 0)
    half = width // 2
    index = jnp.where(lane < half, lane, lane - half).astype(F32)
    freq = jnp.exp(-math.log(10000.0) * index / half)
    times = jnp.zeros((8, width), jnp.int32)
    for m in range(4):
        times = jnp.where(row == m, times_ref[m], times)
    angle = times.astype(F32) * freq
    emb = jnp.where(lane < half, jnp.sin(angle), jnp.cos(angle)).astype(BF)
    film = jnp.dot(emb, film_ref[...], preferred_element_type=F32)
    high = film.astype(BF).astype(F32)
    rows = jnp.concatenate([high[0:4], (film - high)[0:4], jnp.zeros((8, width), F32)], axis=0)
    rows = jnp.concatenate([rows.astype(BF), jnp.zeros((FILM_ROWS, 3 * width), BF)], axis=1)
    pack[0:width] = held
    pack[width:] = rows
    z = lax.axis_index("frame") // 2
    for d in range(levels):
        for k in range(2):
            at = pl.multiple_of(((z ^ d) * 2 + k) * LANES, LANES)
            outs[d][k] = x_ref[:, pl.ds(at, LANES)]


def pack_and_cut(times, own, taps, projection, film_weight, levels):
    width = own.shape[0]
    vmem = pl.BlockSpec(memory_space=pltpu.VMEM)
    return pl.pallas_call(
        functools.partial(pack_kernel, levels),
        out_shape=[pltpu.VMEM((2, width, LANES), BF)] * levels
        + [pltpu.VMEM((width + FILM_ROWS, 4 * width), BF)],
        in_specs=[pl.BlockSpec(memory_space=pltpu.SMEM)] + [vmem] * 4,
        out_specs=[vmem] * (levels + 1),
        name="pack",
    )(times, own, taps, projection, film_weight)


def pick_kernel(*refs):
    other = 1 - lax.axis_index("segment") % 2
    for n, block in enumerate(refs[:-1]):
        refs[-1][n] = block[other]


def pick_others(blocks):
    vmem = pl.BlockSpec(memory_space=pltpu.VMEM)
    return pl.pallas_call(
        pick_kernel,
        out_shape=pltpu.VMEM((len(blocks), *blocks[0].shape[1:]), BF),
        in_specs=[vmem] * len(blocks),
        out_specs=vmem,
        name="pick",
    )(*pin(blocks, pltpu.VMEM))


def join_kernel(parts, *refs):
    blocks, out, joined, sem = refs[: len(parts)], *refs[len(parts) :]
    frame = lax.axis_index("frame")
    z, x = frame // 2, frame % 2
    stores = []
    step = joined.shape[0] // JOIN_STEPS
    for low in range(0, joined.shape[0], step):
        rows = pl.ds(low, step)
        for block, (d, halves) in zip(blocks, parts, strict=True):
            for n, k in enumerate(halves):
                at = pl.multiple_of(((z ^ d) * 2 + (x ^ k)) * LANES, LANES)
                joined[rows, pl.ds(at, LANES)] = block[n, rows]
        stores.append(pltpu.make_async_copy(joined.at[rows], out.at[rows], sem.at[low // step]))
        stores[-1].start()
    for store in stores:
        store.wait()


def join_blocks(blocks, parts):
    width = blocks[0].shape[1]
    columns = sum(len(halves) for _, halves in parts) * LANES
    vmem = pl.BlockSpec(memory_space=pltpu.VMEM)
    return pl.pallas_call(
        functools.partial(join_kernel, parts),
        out_shape=jax.ShapeDtypeStruct((width, columns), BF),
        in_specs=[vmem] * len(blocks),
        out_specs=pl.BlockSpec(memory_space=pltpu.HBM),
        scratch_shapes=[
            pltpu.VMEM((width, columns), BF),
            pltpu.SemaphoreType.DMA((JOIN_STEPS,)),
        ],
        name="join",
    )(*pin(blocks, pltpu.VMEM))


def sections_kernel(dests, levels, width, loaded, *refs):
    refs = list(refs)

    def take(count):
        taken = refs[:count]
        del refs[:count]
        return taken

    turned, (swapped,) = take(len(loaded)), take(1)
    packs = take(4)
    skip_in, gain_ref = take(2)
    kept, given = take(2)
    weights, skip, around, with_one, with_first, two, three = take(7)
    sem_w, sem_s = take(2)
    y, core, z, x = place()
    clip = 2 * y + x
    segment = 2 * y + core
    frames = 2 * levels

    def load_weights(s):
        for b in range(4):

            @pl.when(segment ^ s == b)
            def _():
                pltpu.make_async_copy(packs[b], weights.at[s], sem_w.at[s]).start()

    def wait_weights(s):
        pltpu.make_async_copy(packs[0], weights.at[s], sem_w.at[s]).wait()

    for s in range(4):
        load_weights(s)
    skip_load = pltpu.make_async_copy(skip_in, skip, sem_s)
    skip_load.start()

    def lanes_of(d, k):
        slot = 2 * (z ^ d) + (core ^ k)
        return pl.ds(pl.multiple_of(slot * LANES, LANES), LANES)

    def span(f, count=1):
        return slice(f * LANES, (f + count) * LANES)

    zeros = jnp.zeros((width, LANES), BF)
    around[:, span(0)] = zeros
    around[:, span(frames + 1)] = zeros
    for ref in (with_one, with_first):
        ref[0:64, :] = jnp.zeros((64, frames * LANES), BF)

    def column_of(rows, chosen):
        at = lax.broadcasted_iota(jnp.int32, (16, LANES), 0)
        hit = functools.reduce(jnp.logical_or, [at == c for c in chosen])
        return lax.dot_general(
            rows,
            jnp.where(hit, 1.0, 0.0).astype(BF),
            (((0,), (0,)), ((), ())),
            preferred_element_type=F32,
        )

    gains = []
    rest = gain_ref[...]
    for _ in range(3):
        gains.append(rest.astype(BF).astype(F32))
        rest = rest - gains[-1]
    gains = jnp.concatenate(gains + [jnp.zeros_like(rest)], axis=0).astype(BF)

    one, zero = with_one.at[64 + width :, :], with_first.at[64 + width :, :]
    for n, d in enumerate(loaded):
        for k in range(2):
            zero[:, lanes_of(d, k)] = turned[n][core] if k == 0 else swapped[n]

    gain_columns = [column_of(gains, [s, 4 + s, 8 + s]) for s in range(4)]
    for s in range(4):
        source, target = ((zero, one), (one, two), (two, three), (three, None))[s]
        gain = gain_columns[s]
        values = source[...].astype(F32)
        scale = lax.rsqrt(jnp.mean(values * values, axis=0, keepdims=True) + EPS)
        wide = jnp.concatenate([gain] * frames, axis=1)
        around[:, span(1, frames)] = (values * scale * wide).astype(BF)
        if s == 0:
            wait_weights(0)
        if s == 1:
            for later in range(1, 4):
                wait_weights(later)
            skip_load.wait()
            turned_skip = [skip[n].T for n in range(2)]
        half = 0.5 + 0.5 * column_of(weights[s, width:, 0:width], [clip, 4 + clip])
        half = jnp.concatenate([half] * frames, axis=1)
        three_frames = jnp.concatenate(
            [around[:, span(tau, frames)] for tau in range(3)]
            + [jnp.zeros((64, frames * LANES), BF)],
            axis=0,
        )
        mixed = jnp.dot(
            weights[s, 0:width, 0 : 3 * width + 64], three_frames, preferred_element_type=F32
        )
        mixed = mixed * half
        beside = with_first if s == 3 else with_one
        beside[64 : 64 + width, :] = (mixed * (1.0 + jnp.tanh(mixed))).astype(BF)
        projection = weights[s, 0:width, 3 * width - 64 :]
        right = beside[0 : 64 + width, :]
        if s >= 2:
            projection = jnp.concatenate([projection, turned_skip[s - 2]], axis=1)
            right = beside[...]
        total = source[...].astype(F32)
        total = (total + jnp.dot(projection, right, preferred_element_type=F32)).astype(BF)
        if s < 3:
            target[...] = total
        else:
            outcome = total
    for c in range(2):

        @pl.when(core == c)
        def _():
            for f in range(frames):
                level = z ^ (f // 2)
                at = sum(jnp.where(level == d, n, 0) for n, d in enumerate(dests))
                (kept, given)[(f + c) % 2][at] = outcome[:, span(f)]


def run_sections(dests, loaded, turned, swapped, weights, skip, gain):
    levels = lax.axis_size("frame") // 2
    frames = 2 * levels
    width = gain.shape[1]
    columns = frames * LANES
    vmem = pl.BlockSpec(memory_space=pltpu.VMEM)
    blocks = [*turned, swapped]
    places = [pltpu.VMEM, pltpu.HBM, pltpu.VMEM, pltpu.VMEM, pltpu.HBM]
    inputs = [pin([a], place)[0] for a, place in zip([*weights, skip], places, strict=True)]
    return pl.pallas_call(
        functools.partial(sections_kernel, dests, levels, width, loaded),
        out_shape=[pltpu.VMEM((len(dests), width, LANES), BF)] * 2,
        in_specs=[vmem] * len(blocks)
        + [pl.BlockSpec(memory_space=place) for place in places]
        + [vmem],
        out_specs=[vmem] * 2,
        scratch_shapes=[
            pltpu.VMEM((4, width + FILM_ROWS, 4 * width), BF),
            pltpu.VMEM((2, width, width), BF),
            pltpu.VMEM((width, columns + 2 * LANES), BF),
            pltpu.VMEM((2 * width + 64, columns), BF),
            pltpu.VMEM((2 * width + 64, columns), BF),
            pltpu.VMEM((width, columns), BF),
            pltpu.VMEM((width, columns), BF),
            pltpu.SemaphoreType.DMA((4,)),
            pltpu.SemaphoreType.DMA,
        ],
        compiler_params=pltpu.CompilerParams(vmem_limit_bytes=40 << 20),
        cost_estimate=pl.CostEstimate(
            flops=columns * 2 * 18 * width * width, bytes_accessed=4 << 20, transcendentals=0
        ),
        name="sections",
    )(*pin(blocks, pltpu.VMEM), *inputs, gain)


IN_ORDER = (2, 3, 1, 0)
OUT_ORDER = (2, 3, 1, 0)
OUT_PARTS = ((0, (0, 1)), (1, (0, 1)), (3, (1,)), (2, (1,)), (3, (0,)), (2, (0,)))


def block_shards(clips, timesteps, gain, temporal_weight, film_weight, out_weight, skip_weight):
    levels = lax.axis_size("frame") // 2

    *cut, pack0 = pack_and_cut(
        timesteps, clips[0, 0], temporal_weight[0], out_weight[0], film_weight[0], levels
    )
    pack2 = swap_planes(pack0)
    turned = [turn(cut[d], d) for d in IN_ORDER]
    pack1 = swap_cores(pack0)
    picked = pick_others(turned)
    pack2, picked = lax.optimization_barrier((pack2, picked))
    swapped = swap_cores(picked)
    pack3 = swap_cores(pack2)

    weights = [pack0, pack1, pack2, pack3]
    kept, given = run_sections(
        OUT_ORDER, IN_ORDER, turned, swapped, weights, skip_weight, gain
    )
    swapped = swap_cores(given)
    back = []
    for d, halves in OUT_PARTS:
        n = OUT_ORDER.index(d)
        back.append(turn(jnp.stack([(kept, swapped)[k][n] for k in halves]), d))
    return join_blocks(back, OUT_PARTS)[None, None]


def solution(mesh):
    placed = (
        P("segment", "frame", None, None),
        P(),
        P(),
        P("segment", None, None, None),
        P("segment", None, None),
        P("segment", None, None),
        P(),
    )

    def run(*arrays):
        clips, gain = arrays[0], arrays[2]
        split = mesh.shape["frame"]
        fits = (
            clips.shape[1] == split == 8
            and clips.shape[3] == split * LANES
            and clips.shape[2] % 64 == 0
            and clips.shape[0] == gain.shape[0] == mesh.shape["segment"] == 4
        )
        return jax.shard_map(
            block_shards if fits else plain_shards,
            mesh=mesh,
            in_specs=placed,
            out_specs=P("segment", "frame", None, None),
            check_vma=False,
        )(*arrays)

    return run
```
